128 devices in a mesh: wide: 32 (over x, z, core), narrow: 4 (over y).
Axes of the slice: x: 4, y: 4, z: 4, core: 2. Of those that a mesh axis runs over, the one named last changes fastest.
Arguments:
- deltas: bfloat16 [32, 4718592], P('wide', 'narrow'), may hold values from -64 to 64
- sample_counts: int32 [32], replicated, may hold values from 200 to 4999
- momentum: float32 [4718592], P('narrow'), may hold values from -3 to 3
- weights: float32 [4718592], P('narrow'), may hold values from -6 to 6
Outputs:
- new_weights: float32 [4718592], P('narrow')
- new_momentum: float32 [4718592], P('narrow')
The draws below stay inside these ranges and needn't reach their ends.
All inputs are finite; a program needn't handle non-finite values.
Results may differ from the reference program's by a relative error of at most 0.0003.
Values may be sent and summed in bfloat16 or wider, within the bound.
No kernel may reach another device: no remote copies, remote signals or barrier semaphores. Data moves between devices by JAX's collectives and lax.ppermute only.
A program may use at most 128 MiB of HBM per device.

```python
import jax
import jax.numpy as jnp
from jax import lax

ITERS = 3
CLIENTS = 32
PARAMS = 4718592


def draw_deltas(key, part):
    key = jax.random.fold_in(key, 11)
    keys = jax.random.split(key, 5)
    region_len = PARAMS // 512
    region_index = jnp.arange(PARAMS) // region_len
    client_scale = jnp.exp(jax.random.uniform(keys[0], (CLIENTS, 1), jnp.float32, jnp.log(0.25), jnp.log(4.0)))
    region_scale = jnp.exp(jax.random.uniform(keys[1], (CLIENTS, 512), jnp.float32, -0.7, 0.7))
    ramp = jnp.sqrt(1.0 + 2.0 * jnp.arange(PARAMS).astype(jnp.float32) / PARAMS)
    common = jax.random.truncated_normal(keys[2], -4.0, 4.0, (PARAMS,), jnp.float32)
    noise = jax.random.truncated_normal(keys[3], -4.0, 4.0, (CLIENTS, PARAMS), jnp.float32)
    common_weight = 0.3
    spikes = jax.random.uniform(keys[4], (CLIENTS, PARAMS), jnp.float32) < 1.0 / 2000.0
    noise = noise * jnp.where(spikes, 40.0, 1.0)
    values = client_scale * region_scale[:, region_index] * ramp[None, :] * noise + common_weight * common[None, :]
    values = jnp.clip(values, -64.0, 64.0)
    return values.astype(jnp.bfloat16)


def touch_ends(entries, rng, smallest, top_value):
    spot = [jax.random.randint(jax.random.fold_in(rng, axis), (), 0, length) for axis, length in enumerate(entries.shape)]
    longest = entries.shape.index(max(entries.shape))
    neighbour = spot[:longest] + [(spot[longest] + 1) % entries.shape[longest]] + spot[longest + 1:]
    return entries.at[tuple(spot)].set(smallest).at[tuple(neighbour)].set(top_value)


def block_levels(rng, extent, shards, least, high):
    factor_of = 1.0
    for axis_at, shards_of in shards:
        steps = jax.random.uniform(jax.random.fold_in(jax.random.fold_in(rng, 6), axis_at), (shards_of,), jnp.float32, least / len(shards), high / len(shards))
        factor_of = factor_of * jnp.repeat(jnp.exp(steps), extent[axis_at] // shards_of).reshape((-1,) + (1,) * (len(extent) - 1 - axis_at))
    return factor_of


def scatter_about(rng, shape, scale, reach, cuts=(), dtype=jnp.bfloat16):
    factor_of = block_levels(rng, shape, cuts, -0.22, 0.18) if cuts else 1.0
    values = jax.random.normal(rng, shape, jnp.float32) * scale * factor_of
    return jnp.minimum(jnp.maximum(values, -reach), reach).astype(dtype)


def setup_inputs(seed: int = 0) -> dict:
    splits = jax.random.split(jax.random.key(seed), 5)
    deltas = draw_deltas(jax.random.fold_in(splits[4], 71), 0)
    sample_counts = touch_ends(jax.random.randint(splits[1], (CLIENTS,), 200, 5000), jax.random.fold_in(splits[1], 1), 200, 4999).astype(jnp.int32)
    momentum = scatter_about(splits[2], (PARAMS,), 0.5, 3.0, ((0, 4),), jnp.float32)
    weights = scatter_about(splits[3], (PARAMS,), 1.0, 6.0, ((0, 4),), jnp.float32)
    return {"deltas": deltas, "sample_counts": sample_counts, "momentum": momentum, "weights": weights}


NU_SQUARE = 1.0
MOMENTUM_RATE = 0.9
SERVER_RATE = 1.0

def reference(deltas, sample_counts, momentum, weights):
    counts = sample_counts.astype(jnp.float32)
    client_share = counts / jnp.sum(counts)

    def weighted(coefficients):

        def step(accum, pair):
            client_row, factor = pair
            return (accum + factor * client_row.astype(jnp.float32), None)
        accum, _ = lax.scan(step, jnp.zeros((deltas.shape[1],), jnp.float32), (deltas, coefficients))
        return accum

    def distance(median):
        return lax.map(lambda client_row: jnp.sum(jnp.square(client_row.astype(jnp.float32) - median)), deltas)
    median = weighted(client_share)
    for sweep in range(ITERS):
        distances = jnp.sqrt(distance(median) + NU_SQUARE)
        beta_weights = client_share / distances
        median = weighted(beta_weights) / jnp.sum(beta_weights)
    new_momentum = MOMENTUM_RATE * momentum + median
    new_weights = weights + SERVER_RATE * new_momentum
    return (new_weights, new_momentum)
```

```python
import jax
import jax.numpy as jnp
from jax import lax
from jax.experimental import pallas as pl
from jax.experimental.pallas import tpu as pltpu
from jax.sharding import PartitionSpec as P

ITERS = 3


NU_SQUARE = 1.0
MOMENTUM_RATE = 0.9
SERVER_RATE = 1.0

LANES = 128
GROUP = 16
SENT_TOP = 16376.0
SMALLEST_NORM = 1e-17
SAFE_SHARE = 1.0 / 256.0
VMEM = 48 << 20


def pack_kernel(flat_ref, packed_ref):
    packed_ref[...] = flat_ref[...].reshape(packed_ref.shape)


def pack(deltas, clients):
    entries = deltas.shape[1]
    rows = entries // LANES
    steps = 2
    packed = pl.pallas_call(
        pack_kernel,
        grid=(steps,),
        in_specs=[pl.BlockSpec((1, entries // steps), lambda i: (0, i))],
        out_specs=pl.BlockSpec((rows // steps, LANES), lambda i: (i, 0)),
        out_shape=jax.ShapeDtypeStruct((rows, LANES), deltas.dtype),
        compiler_params=pltpu.CompilerParams(vmem_limit_bytes=VMEM),
    )(deltas)
    return packed.reshape(clients, rows // clients, LANES)


def gram_kernel(x_ref, out_ref):
    clients, rows, _ = x_ref.shape
    wide = clients * GROUP
    y = jnp.concatenate(
        [x_ref[:, pl.ds(GROUP * k, GROUP), :].reshape(wide, LANES) for k in range(rows // GROUP)], axis=1
    )
    products = lax.dot_general(y, y, (((1,), (1,)), ((), ())), preferred_element_type=jnp.float32)
    row = lax.broadcasted_iota(jnp.int32, products.shape, 0)
    column = lax.broadcasted_iota(jnp.int32, products.shape, 1)
    products = jnp.where((row & (GROUP - 1)) == (column & (GROUP - 1)), products, 0.0)
    summed = products.reshape(clients, GROUP, wide).sum(axis=1)
    owner = lax.broadcasted_iota(jnp.int32, (wide, LANES), 0) // GROUP
    lane = lax.broadcasted_iota(jnp.int32, (wide, LANES), 1)
    gram = jnp.zeros((8, LANES), jnp.float32)
    for b in range(clients // 8):
        place = jnp.where(lane == owner + clients * b, 1.0, 0.0)
        gram = gram + jnp.dot(
            summed[8 * b : 8 * b + 8], place, precision=lax.Precision.HIGHEST, preferred_element_type=jnp.float32
        )
    out_ref[...] = jnp.broadcast_to(gram[None], out_ref.shape)


def gram_copies(x, copies):
    return pl.pallas_call(
        gram_kernel,
        out_shape=jax.ShapeDtypeStruct((copies, 8, LANES), jnp.float32),
        compiler_params=pltpu.CompilerParams(vmem_limit_bytes=VMEM),
    )(x)


def median_kernel(grams_ref, counts_ref, x_ref, median_ref, facts_ref, beta_ref):
    clients, rows, _ = x_ref.shape
    packed = jnp.sum(grams_ref[...], axis=0)
    lane = lax.broadcasted_iota(jnp.int32, (clients, LANES), 1)
    row = lax.broadcasted_iota(jnp.int32, (clients, LANES), 0)
    gram = jnp.concatenate(
        [packed] + [pltpu.roll(packed, LANES - clients * b, 1) for b in range(1, clients // 8)], axis=0
    )
    gram = jnp.where(lane < clients, gram, 0.0)
    square = jnp.where(lane == row, gram, 0.0).sum(axis=0, keepdims=True)
    norm = jnp.sqrt(square)

    def as_column(values):
        return jnp.where(lane == row, values, 0.0).sum(axis=1, keepdims=True)

    counts = counts_ref[...]
    share = counts / counts.sum(axis=1, keepdims=True)
    beta = share
    safe = jnp.ones((1, 1), jnp.float32)
    for sweep in range(ITERS):
        column = as_column(beta)
        inner = (gram * column).sum(axis=0, keepdims=True)
        median_square = (inner * beta).sum(axis=1, keepdims=True)
        mean_norm = (norm * beta).sum(axis=1, keepdims=True)
        distance = square - 2.0 * inner + median_square + NU_SQUARE
        scale = norm + mean_norm
        margin = jnp.where(lane[:1] < clients, distance - SAFE_SHARE * (scale * scale), 1.0)
        safe = jnp.minimum(safe, margin.min(axis=1, keepdims=True))
        beta = share / jnp.sqrt(jnp.maximum(distance, NU_SQUARE))
        beta = beta / beta.sum(axis=1, keepdims=True)
    largest = jnp.maximum((norm * beta).sum(axis=1, keepdims=True), SMALLEST_NORM)
    up = SENT_TOP / largest
    fact = lax.broadcasted_iota(jnp.int32, facts_ref.shape, 0)
    facts_ref[...] = jnp.where(fact == 0, safe, largest * (1.0 / SENT_TOP))
    beta_ref[...] = jnp.broadcast_to(as_column(beta) * up, beta_ref.shape)
    block = 48

    def step(k, carry):
        at = pl.ds(pl.multiple_of(k * block, block), block)
        total = jnp.zeros((block, LANES), jnp.float32)
        for c in range(clients):
            total = total + beta_ref[c : c + 1, :] * x_ref[c, at, :].astype(jnp.float32)
        median_ref[at, :] = total
        return carry

    lax.fori_loop(0, rows // block, step, 0)


def median_of(grams, counts, x):
    clients, rows, _ = x.shape
    return pl.pallas_call(
        median_kernel,
        out_shape=(
            jax.ShapeDtypeStruct((rows, LANES), jnp.float32),
            jax.ShapeDtypeStruct((8, LANES), jnp.float32),
        ),
        scratch_shapes=[pltpu.VMEM((clients, LANES), jnp.float32)],
        compiler_params=pltpu.CompilerParams(vmem_limit_bytes=VMEM),
    )(grams, counts, x)


def direct(x, counts):
    share = counts / jnp.sum(counts)
    wide = x.astype(jnp.float32)

    def weighted(coefficients):
        return jnp.sum(coefficients[:, None, None] * wide, axis=0)

    median = weighted(share)
    for sweep in range(ITERS):
        squared = lax.psum(jnp.sum(jnp.square(wide - median[None]), axis=(1, 2)), ("wide", "narrow"))
        beta = share / jnp.sqrt(squared + NU_SQUARE)
        beta = beta / jnp.sum(beta)
        median = weighted(beta)
    norm = jnp.sqrt(lax.psum(jnp.sum(jnp.square(wide), axis=(1, 2)), ("wide", "narrow")))
    largest = jnp.maximum(jnp.sum(norm * beta), SMALLEST_NORM)
    return median * (SENT_TOP / largest), largest * (1.0 / SENT_TOP)


def shards(deltas, sample_counts, momentum, weights):
    clients = sample_counts.shape[0]
    counts = sample_counts.astype(jnp.float32)
    padded = jnp.pad(counts, (0, LANES - clients)).reshape(1, LANES)
    x = lax.all_to_all(pack(deltas, clients), "wide", split_axis=0, concat_axis=0, tiled=True)
    devices = lax.axis_size(("wide", "narrow"))
    grams = lax.all_to_all(gram_copies(x, devices), ("wide", "narrow"), split_axis=0, concat_axis=0, tiled=True)
    median, facts = median_of(grams, padded, x)
    median, down = lax.cond(facts[0, 0] > 0.0, lambda: (median, facts[1, 0]), lambda: direct(x, counts))
    sent = median.reshape(-1).astype(jnp.float16)
    gathered = lax.all_gather(sent, "wide", axis=0, tiled=True)
    new_momentum = MOMENTUM_RATE * momentum + gathered.astype(jnp.float32) * down
    new_weights = weights + SERVER_RATE * new_momentum
    return (new_weights, new_momentum)


def solution(mesh):
    placed = (P("wide", "narrow"), P(), P("narrow"), P("narrow"))
    return jax.shard_map(
        shards, mesh=mesh, in_specs=placed, out_specs=(P("narrow"), P("narrow")), check_vma=False
    )
```

```python
import jax
import jax.numpy as jnp
from jax import lax
from jax.experimental import pallas as pl
from jax.experimental.pallas import tpu as pltpu
from jax.sharding import PartitionSpec as P

ITERS = 3


NU_SQUARE = 1.0
MOMENTUM_RATE = 0.9
SERVER_RATE = 1.0

LANES = 128
GROUP = 16
BLOCK = 48
SHARED = 24
TOP = 32000.0
SMALLEST = 2.0**-100
SAFE_SHARE = 1.0 / 256.0
VMEM = 24 << 20
SIDE = 4


def params(**more):
    return pltpu.CompilerParams(vmem_limit_bytes=VMEM, **more)


def pack_kernel(flat_ref, packed_ref):
    packed_ref[...] = flat_ref[...].reshape(packed_ref.shape)


def pack(deltas, clients):
    entries = deltas.shape[1]
    rows = entries // LANES
    steps = 2
    packed = pl.pallas_call(
        pack_kernel,
        grid=(steps,),
        in_specs=[pl.BlockSpec((1, entries // steps), lambda i: (0, i))],
        out_specs=pl.BlockSpec((rows // steps, LANES), lambda i: (i, 0)),
        out_shape=jax.ShapeDtypeStruct((rows, LANES), deltas.dtype),
        compiler_params=params(),
    )(deltas)
    return packed.reshape(clients, rows // clients, LANES)


def gram_kernel(x_ref, out_ref):
    clients, rows, _ = x_ref.shape
    wide = clients * GROUP
    y = jnp.concatenate(
        [x_ref[:, pl.ds(GROUP * k, GROUP), :].reshape(wide, LANES) for k in range(rows // GROUP)], axis=1
    )
    products = lax.dot_general(y, y, (((1,), (1,)), ((), ())), preferred_element_type=jnp.float32)
    row = lax.broadcasted_iota(jnp.int32, products.shape, 0)
    column = lax.broadcasted_iota(jnp.int32, products.shape, 1)
    products = jnp.where((row & (GROUP - 1)) == (column & (GROUP - 1)), products, 0.0)
    summed = products.reshape(clients, GROUP, wide).sum(axis=1)
    owner = lax.broadcasted_iota(jnp.int32, (wide, LANES), 0) // GROUP
    lane = lax.broadcasted_iota(jnp.int32, (wide, LANES), 1)
    place = jnp.where((lane & (clients - 1)) == owner, 1.0, 0.0)
    gram = jnp.dot(summed, place, precision=lax.Precision.HIGHEST, preferred_element_type=jnp.float32)
    row = lax.broadcasted_iota(jnp.int32, gram.shape, 0)
    lane = lax.broadcasted_iota(jnp.int32, gram.shape, 1)
    for j in range(out_ref.shape[1]):
        other = (lane - (4 * j + lane // clients)) & (clients - 1)
        diagonals = jnp.where(row == other, gram, 0.0).sum(axis=0, keepdims=True)
        out_ref[:, j] = jnp.broadcast_to(diagonals[None], (out_ref.shape[0], 1, LANES))


def gram_copies(x, copies):
    clients, rows, _ = x.shape
    return pl.pallas_call(
        gram_kernel,
        out_shape=jax.ShapeDtypeStruct((copies, clients // 8 + 1, 1, LANES), jnp.float32),
        compiler_params=params(),
    )(x)


def encode(total):
    values, exponents = [], []
    for at in range(0, BLOCK, SHARED):
        part = total[at : at + SHARED]
        largest = jnp.maximum(jnp.abs(part).max(axis=0, keepdims=True), SMALLEST)
        exponent = jnp.ceil(jnp.log2(largest))
        values.append(jnp.round(part * (TOP * jnp.exp2(-exponent))))
        exponents.append(exponent)
    return jnp.concatenate(values, axis=0).astype(jnp.int32).astype(jnp.int16), exponents


def encode_into(piece_ref, exponent_ref, rows, total_of):
    exponent_ref[...] = jnp.zeros_like(exponent_ref)

    def step(k, carry):
        at = pl.ds(pl.multiple_of(k * BLOCK, BLOCK), BLOCK)
        values, exponents = encode(total_of(at))
        piece_ref[at, :] = values
        for i, exponent in enumerate(exponents):
            exponent_ref[pl.ds(len(exponents) * k + i, 1), :] = exponent
        return carry

    lax.fori_loop(0, rows // BLOCK, step, 0)
    piece_ref[rows : rows + GROUP, :] = exponent_ref[...].astype(jnp.int32).astype(jnp.int16)


def encode_kernel(median_ref, piece_ref, exponent_ref):
    encode_into(piece_ref, exponent_ref, median_ref.shape[0], lambda at: median_ref[at, :])


def encoded(median):
    rows, _ = median.shape
    return pl.pallas_call(
        encode_kernel,
        out_shape=jax.ShapeDtypeStruct((rows + GROUP, LANES), jnp.int16),
        scratch_shapes=[pltpu.VMEM((GROUP, LANES), jnp.float32)],
        compiler_params=params(),
    )(median)


def median_kernel(grams_ref, counts_ref, x_ref, piece_ref, safe_ref, beta_ref, exponent_ref):
    clients, rows, _ = x_ref.shape
    summed = jnp.sum(grams_ref[...], axis=0)
    lane = lax.broadcasted_iota(jnp.int32, (clients, LANES), 1)
    row = lax.broadcasted_iota(jnp.int32, (clients, LANES), 0)
    behind = jnp.where(lane < clients, (lane - row) & (clients - 1), clients)
    half = jnp.zeros((clients, LANES), jnp.float32)
    for k in range(clients // 2 + 1):
        diagonal = summed[k // 4]
        if k % 4:
            diagonal = pltpu.roll(diagonal, LANES - clients * (k % 4), 1)
        half = jnp.where(behind == k, diagonal, half)
    identity = jnp.where(lane == row, 1.0, 0.0)
    turned = lax.dot_general(
        half,
        identity,
        (((0,), (0,)), ((), ())),
        precision=lax.Precision.HIGHEST,
        preferred_element_type=jnp.float32,
    )[:clients]
    gram = jnp.where(behind <= clients // 2, half, turned)
    gram = jnp.where(lane < clients, gram, 0.0)
    square = jnp.where(lane == row, gram, 0.0).sum(axis=0, keepdims=True)
    norm = jnp.sqrt(square)

    def as_column(values):
        return jnp.where(lane == row, values, 0.0).sum(axis=1, keepdims=True)

    counts = counts_ref[...]
    share = counts / counts.sum(axis=1, keepdims=True)
    beta = share
    safe = jnp.ones((1, 1), jnp.float32)
    for sweep in range(ITERS):
        column = as_column(beta)
        inner = (gram * column).sum(axis=0, keepdims=True)
        median_square = (inner * beta).sum(axis=1, keepdims=True)
        mean_norm = (norm * beta).sum(axis=1, keepdims=True)
        distance = square - 2.0 * inner + median_square + NU_SQUARE
        scale = norm + mean_norm
        margin = jnp.where(lane[:1] < clients, distance - SAFE_SHARE * (scale * scale), 1.0)
        safe = jnp.minimum(safe, margin.min(axis=1, keepdims=True))
        beta = share / jnp.sqrt(jnp.maximum(distance, NU_SQUARE))
        beta = beta / beta.sum(axis=1, keepdims=True)
    safe_ref[0] = jnp.where(safe[0, 0] > 0.0, 1, 0)
    beta_ref[...] = jnp.broadcast_to(as_column(beta), beta_ref.shape)

    def total_of(at):
        total = jnp.zeros((BLOCK, LANES), jnp.float32)
        for c in range(clients):
            total = total + beta_ref[c : c + 1, :] * x_ref[c, at, :].astype(jnp.float32)
        return total

    encode_into(piece_ref, exponent_ref, rows, total_of)


def median_of(grams, counts, x):
    clients, rows, _ = x.shape
    return pl.pallas_call(
        median_kernel,
        out_shape=(
            jax.ShapeDtypeStruct((rows + GROUP, LANES), jnp.int16),
            jax.ShapeDtypeStruct((1,), jnp.int32),
        ),
        out_specs=(pl.BlockSpec(memory_space=pltpu.VMEM), pl.BlockSpec(memory_space=pltpu.SMEM)),
        scratch_shapes=[pltpu.VMEM((clients, LANES), jnp.float32), pltpu.VMEM((GROUP, LANES), jnp.float32)],
        compiler_params=params(),
    )(grams, counts, x)


def update_kernel(parts, me_ref, *refs):
    quads = refs[: len(parts)]
    momentum_ref, weights_ref = refs[len(parts) : len(parts) + 2]
    new_momentum_ref, new_weights_ref, held, in_sem, out_sem = refs[-5:]
    rows = momentum_ref.shape[1]
    me = me_ref[0]
    x, z = me // (2 * SIDE), (me // 2) % SIDE

    def place(part, near_slot):
        flip, far_slot = parts[part]
        core = (me + flip) % 2
        near = jnp.where(core == 0, z, x)
        far = jnp.where(core == 0, x, z)
        near_at = (near + SIDE - near_slot) % SIDE
        far_at = (far + SIDE - far_slot) % SIDE
        return jnp.where(core == 0, far_at * SIDE + near_at, near_at * SIDE + far_at) * 2 + core

    def fetch(part, near_slot, i):
        slot = SIDE * part + near_slot
        source = (momentum_ref, weights_ref)[i]
        return pltpu.make_async_copy(source.at[place(part, near_slot)], held.at[slot, i], in_sem.at[slot, i])

    def store(part, near_slot, i):
        slot = SIDE * part + near_slot
        target = (new_momentum_ref, new_weights_ref)[i]
        return pltpu.make_async_copy(held.at[slot, i], target.at[place(part, near_slot)], out_sem.at[slot, i])

    def each(part, act):
        def step(near_slot, carry):
            for i in range(2):
                act(part, near_slot, i)
            return carry

        lax.fori_loop(0, SIDE, step, 0)

    for part in range(len(parts)):
        each(part, lambda *at: fetch(*at).start())
    for part in range(len(parts)):
        quad = quads[part]

        def work(near_slot, carry):
            slot = SIDE * part + near_slot
            for i in range(2):
                fetch(part, near_slot, i).wait()
            exponents = quad[near_slot, rows : rows + GROUP, :].astype(jnp.int32).astype(jnp.float32)
            scales = jnp.exp2(exponents) * (1.0 / TOP)
            for at in range(0, rows, BLOCK):
                values = quad[near_slot, at : at + BLOCK, :].astype(jnp.int32).astype(jnp.float32)
                for low in range(0, BLOCK, SHARED):
                    i = (at + low) // SHARED
                    block = pl.ds(at + low, SHARED)
                    median = values[low : low + SHARED] * scales[i : i + 1]
                    moved = MOMENTUM_RATE * held[slot, 0, block, :] + median
                    held[slot, 0, block, :] = moved
                    held[slot, 1, block, :] = held[slot, 1, block, :] + SERVER_RATE * moved
            for i in range(2):
                store(part, near_slot, i).start()
            return carry

        lax.fori_loop(0, SIDE, work, 0)
    for part in range(len(parts)):
        each(part, lambda *at: store(*at).wait())


def update(parts, me, quads, momentum, weights, made=()):
    pieces, rows, _ = momentum.shape
    vmem, hbm = pl.BlockSpec(memory_space=pltpu.VMEM), pl.BlockSpec(memory_space=pltpu.HBM)
    shape = pltpu.HBM(momentum.shape, momentum.dtype)
    in_hbm = [pltpu.with_memory_space_constraint(array, pltpu.HBM) for array in (momentum, weights, *made)]
    slots = SIDE * len(parts)
    return pl.pallas_call(
        lambda *refs: update_kernel(parts, *refs),
        in_specs=[pl.BlockSpec(memory_space=pltpu.SMEM)] + [vmem] * len(quads) + [hbm] * len(in_hbm),
        out_specs=(hbm, hbm),
        out_shape=(shape, shape),
        scratch_shapes=[
            pltpu.VMEM((slots, 2, rows, LANES), jnp.float32),
            pltpu.SemaphoreType.DMA((slots, 2)),
            pltpu.SemaphoreType.DMA((slots, 2)),
        ],
        input_output_aliases={1 + len(quads) + 2 + i: i for i in range(len(made))},
        compiler_params=params(),
        cost_estimate=pl.CostEstimate(
            flops=slots * rows * LANES * 6, bytes_accessed=4 * slots * rows * LANES * 4, transcendentals=0
        ),
    )(me, *quads, *in_hbm)


def along(step, shift):
    pairs = []
    for x in range(SIDE):
        for z in range(SIDE):
            for core in range(2):
                if (core == 0) == (step == 0):
                    to_x, to_z = x, (z + shift) % SIDE
                else:
                    to_x, to_z = (x + shift) % SIDE, z
                pairs.append(((x * SIDE + z) * 2 + core, (to_x * SIDE + to_z) * 2 + core))
    return pairs


def direct(x, counts):
    share = counts / jnp.sum(counts)
    wide = x.astype(jnp.float32)

    def weighted(coefficients):
        return jnp.sum(coefficients[:, None, None] * wide, axis=0)

    median = weighted(share)
    for sweep in range(ITERS):
        squared = lax.psum(jnp.sum(jnp.square(wide - median[None]), axis=(1, 2)), ("wide", "narrow"))
        beta = share / jnp.sqrt(squared + NU_SQUARE)
        median = weighted(beta) / jnp.sum(beta)
    return median


def shards(deltas, sample_counts, momentum, weights):
    clients = sample_counts.shape[0]
    counts = sample_counts.astype(jnp.float32)
    padded = jnp.pad(counts, (0, LANES - clients)).reshape(1, LANES)
    me = lax.axis_index("wide").astype(jnp.int32).reshape(1)
    x = lax.all_to_all(pack(deltas, clients), "wide", split_axis=0, concat_axis=0, tiled=True)
    devices = lax.axis_size(("wide", "narrow"))
    grams = lax.all_to_all(gram_copies(x, devices), ("wide", "narrow"), split_axis=0, concat_axis=0, tiled=True)
    flat = momentum.shape
    blocks = (clients, momentum.shape[0] // clients // LANES, LANES)
    momentum, weights = momentum.reshape(blocks), weights.reshape(blocks)
    piece, safe = median_of(grams, padded, x)

    def again(state):
        return jnp.int32(1), encoded(direct(x, counts))

    _, piece = lax.while_loop(lambda state: state[0] == 0, again, (safe[0], piece))

    near = [piece] + [lax.ppermute(piece, "wide", along(0, shift)) for shift in range(1, SIDE)]
    own = jnp.stack(near)
    ours = [own] + [lax.ppermute(own, "wide", along(1, shift)) for shift in range(1, SIDE)]
    across = [(i, i ^ 1) for i in range(2 * SIDE * SIDE)]
    mine = [lax.ppermute(own, "wide", along(1, shift)) for shift in (1, 3, 2)]
    theirs = lax.ppermute(own, "wide", across)
    made = update([(0, 0), (1, 0)], me, [own, theirs], momentum, weights)
    first, second, *made = lax.optimization_barrier((mine[0], mine[1], *made))
    theirs = [lax.ppermute(quad, "wide", across) for quad in (first, second)]
    made = update([(0, 1), (0, 3)], me, [first, second], momentum, weights, made)
    last, *made = lax.optimization_barrier((mine[2], *made))
    theirs = theirs + [lax.ppermute(last, "wide", across)]
    made = update([(1, 1), (1, 3), (0, 2)], me, [*theirs[:2], last], momentum, weights, made)
    new_momentum, new_weights = update([(1, 2)], me, theirs[2:], momentum, weights, made)
    return (new_weights.reshape(flat), new_momentum.reshape(flat))


def solution(mesh):
    placed = (P("wide", "narrow"), P(), P("narrow"), P("narrow"))
    return jax.shard_map(
        shards, mesh=mesh, in_specs=placed, out_specs=(P("narrow"), P("narrow")), check_vma=False
    )
```

```python
import jax
import jax.numpy as jnp
from jax import lax
from jax.experimental import pallas as pl
from jax.experimental.pallas import tpu as pltpu
from jax.sharding import PartitionSpec as P

ITERS = 3


NU_SQUARE = 1.0
MOMENTUM_RATE = 0.9
SERVER_RATE = 1.0

LANES = 128
GROUP = 16
GRAM_ROWS = 8
BLOCK = 48
SHARED = 24
TOP = 32000.0
SMALLEST = 2.0**-100
SAFE_SHARE = 1.0 / 256.0
VMEM = 24 << 20
SIDE = 4


def params(**more):
    return pltpu.CompilerParams(vmem_limit_bytes=VMEM, **more)


def pack_kernel(flat_ref, packed_ref):
    packed_ref[...] = flat_ref[...].reshape(packed_ref.shape)


def pack(deltas, clients):
    entries = deltas.shape[1]
    rows = entries // LANES
    steps = 2
    packed = pl.pallas_call(
        pack_kernel,
        grid=(steps,),
        in_specs=[pl.BlockSpec((1, entries // steps), lambda i: (0, i))],
        out_specs=pl.BlockSpec((rows // steps, LANES), lambda i: (i, 0)),
        out_shape=jax.ShapeDtypeStruct((rows, LANES), deltas.dtype),
        compiler_params=params(),
    )(deltas)
    return packed.reshape(clients, rows // clients, LANES)


def gram_kernel(x_ref, out_ref):
    clients, rows, _ = x_ref.shape
    wide = clients * GRAM_ROWS
    y = jnp.concatenate(
        [x_ref[:, pl.ds(GRAM_ROWS * k, GRAM_ROWS), :].reshape(wide, LANES) for k in range(rows // GRAM_ROWS)], axis=1
    )
    products = lax.dot_general(y, y, (((1,), (1,)), ((), ())), preferred_element_type=jnp.float32)
    row = lax.broadcasted_iota(jnp.int32, products.shape, 0)
    column = lax.broadcasted_iota(jnp.int32, products.shape, 1)
    products = jnp.where((row & (GRAM_ROWS - 1)) == (column & (GRAM_ROWS - 1)), products, 0.0)
    summed = products.reshape(clients, GRAM_ROWS, wide).sum(axis=1)
    owner = lax.broadcasted_iota(jnp.int32, (wide, LANES), 0) // GRAM_ROWS
    lane = lax.broadcasted_iota(jnp.int32, (wide, LANES), 1)
    place = jnp.where((lane & (clients - 1)) == owner, 1.0, 0.0)
    gram = jnp.dot(summed, place, precision=lax.Precision.HIGHEST, preferred_element_type=jnp.float32)
    row = lax.broadcasted_iota(jnp.int32, gram.shape, 0)
    lane = lax.broadcasted_iota(jnp.int32, gram.shape, 1)
    for j in range(out_ref.shape[1]):
        other = (lane - (4 * j + lane // clients)) & (clients - 1)
        diagonals = jnp.where(row == other, gram, 0.0).sum(axis=0, keepdims=True)
        out_ref[:, j] = jnp.broadcast_to(diagonals[None], (out_ref.shape[0], 1, LANES))


def gram_copies(x, copies):
    clients, rows, _ = x.shape
    return pl.pallas_call(
        gram_kernel,
        out_shape=jax.ShapeDtypeStruct((copies, clients // 8 + 1, 1, LANES), jnp.float32),
        compiler_params=params(),
    )(x)


def encode(total):
    values, exponents = [], []
    for at in range(0, BLOCK, SHARED):
        part = total[at : at + SHARED]
        largest = jnp.maximum(jnp.abs(part).max(axis=0, keepdims=True), SMALLEST)
        exponent = jnp.ceil(jnp.log2(largest))
        values.append(jnp.round(part * (TOP * jnp.exp2(-exponent))))
        exponents.append(exponent)
    return jnp.concatenate(values, axis=0).astype(jnp.int32).astype(jnp.int16), exponents


def encode_into(piece_ref, exponent_ref, rows, total_of):
    exponent_ref[...] = jnp.zeros_like(exponent_ref)

    def step(k, carry):
        at = pl.ds(pl.multiple_of(k * BLOCK, BLOCK), BLOCK)
        values, exponents = encode(total_of(at))
        piece_ref[at, :] = values
        for i, exponent in enumerate(exponents):
            exponent_ref[pl.ds(len(exponents) * k + i, 1), :] = exponent
        return carry

    lax.fori_loop(0, rows // BLOCK, step, 0)
    piece_ref[rows : rows + GROUP, :] = exponent_ref[...].astype(jnp.int32).astype(jnp.int16)


def median_kernel(grams_ref, counts_ref, x_ref, piece_ref, safe_ref, beta_ref, exponent_ref):
    clients, rows, _ = x_ref.shape
    summed = jnp.sum(grams_ref[...], axis=0)
    lane = lax.broadcasted_iota(jnp.int32, (clients, LANES), 1)
    row = lax.broadcasted_iota(jnp.int32, (clients, LANES), 0)
    behind = jnp.where(lane < clients, (lane - row) & (clients - 1), clients)
    half = jnp.zeros((clients, LANES), jnp.float32)
    for k in range(clients // 2 + 1):
        diagonal = summed[k // 4]
        if k % 4:
            diagonal = pltpu.roll(diagonal, LANES - clients * (k % 4), 1)
        half = jnp.where(behind == k, diagonal, half)
    identity = jnp.where(lane == row, 1.0, 0.0)
    turned = lax.dot_general(
        half,
        identity,
        (((0,), (0,)), ((), ())),
        precision=lax.Precision.HIGHEST,
        preferred_element_type=jnp.float32,
    )[:clients]
    gram = jnp.where(behind <= clients // 2, half, turned)
    gram = jnp.where(lane < clients, gram, 0.0)
    square = jnp.where(lane == row, gram, 0.0).sum(axis=0, keepdims=True)
    norm = jnp.sqrt(square)

    square_column = jnp.where(lane == row, gram, 0.0).sum(axis=1, keepdims=True)
    counts = counts_ref[...]
    beta, beta_column = counts, jnp.where(lane == row, counts, 0.0).sum(axis=1, keepdims=True)
    share, share_column = beta, beta_column
    safe = jnp.ones((1, 1), jnp.float32)
    for sweep in range(ITERS):
        part = 1.0 / beta.sum(axis=1, keepdims=True)
        inner = (gram * beta_column).sum(axis=0, keepdims=True)
        inner_column = (gram * beta).sum(axis=1, keepdims=True)
        median_square = (inner * beta).sum(axis=1, keepdims=True) * (part * part)
        mean_norm = (norm * beta).sum(axis=1, keepdims=True) * part
        distance = square - (2.0 * part) * inner + median_square + NU_SQUARE
        distance_column = square_column - (2.0 * part) * inner_column + median_square + NU_SQUARE
        scale = norm + mean_norm
        margin = jnp.where(lane[:1] < clients, distance - SAFE_SHARE * (scale * scale), 1.0)
        safe = jnp.minimum(safe, margin.min(axis=1, keepdims=True))
        beta = share / jnp.sqrt(jnp.maximum(distance, NU_SQUARE))
        beta_column = share_column / jnp.sqrt(jnp.maximum(distance_column, NU_SQUARE))
    beta_column = beta_column / beta.sum(axis=1, keepdims=True)
    safe_ref[0] = jnp.where(safe[0, 0] > 0.0, 1, 0)
    beta_ref[...] = jnp.broadcast_to(beta_column, beta_ref.shape)

    def total_of(at):
        total = jnp.zeros((BLOCK, LANES), jnp.float32)
        for c in range(clients):
            total = total + beta_ref[c : c + 1, :] * x_ref[c, at, :].astype(jnp.float32)
        return total

    encode_into(piece_ref, exponent_ref, rows, total_of)


def median_of(grams, counts, x):
    clients, rows, _ = x.shape
    return pl.pallas_call(
        median_kernel,
        out_shape=(
            jax.ShapeDtypeStruct((rows + GROUP, LANES), jnp.int16),
            jax.ShapeDtypeStruct((1,), jnp.int32),
        ),
        out_specs=(pl.BlockSpec(memory_space=pltpu.VMEM), pl.BlockSpec(memory_space=pltpu.SMEM)),
        scratch_shapes=[pltpu.VMEM((clients, LANES), jnp.float32), pltpu.VMEM((GROUP, LANES), jnp.float32)],
        compiler_params=params(),
    )(grams, counts, x)


def update_kernel(parts, me_ref, *refs):
    quads = refs[: len(parts)]
    momentum_ref, weights_ref = refs[len(parts) : len(parts) + 2]
    new_momentum_ref, new_weights_ref, held, in_sem, out_sem = refs[-5:]
    rows = momentum_ref.shape[1]
    me = me_ref[0]
    x, z = me // (2 * SIDE), (me // 2) % SIDE

    def place(part, near_slot):
        flip, far_slot = parts[part]
        core = (me + flip) % 2
        near = jnp.where(core == 0, z, x)
        far = jnp.where(core == 0, x, z)
        near_at = (near + SIDE - near_slot) % SIDE
        far_at = (far + SIDE - far_slot) % SIDE
        return jnp.where(core == 0, far_at * SIDE + near_at, near_at * SIDE + far_at) * 2 + core

    def fetch(part, near_slot, i):
        slot = SIDE * part + near_slot
        source = (momentum_ref, weights_ref)[i]
        return pltpu.make_async_copy(source.at[place(part, near_slot)], held.at[slot, i], in_sem.at[slot, i])

    def store(part, near_slot, i):
        slot = SIDE * part + near_slot
        target = (new_momentum_ref, new_weights_ref)[i]
        return pltpu.make_async_copy(held.at[slot, i], target.at[place(part, near_slot)], out_sem.at[slot, i])

    def each(part, act):
        def step(near_slot, carry):
            for i in range(2):
                act(part, near_slot, i)
            return carry

        lax.fori_loop(0, SIDE, step, 0)

    for part in range(len(parts)):
        each(part, lambda *at: fetch(*at).start())
    for part in range(len(parts)):
        quad = quads[part]

        def work(near_slot, carry):
            slot = SIDE * part + near_slot
            for i in range(2):
                fetch(part, near_slot, i).wait()
            exponents = quad[near_slot, rows : rows + GROUP, :].astype(jnp.int32).astype(jnp.float32)
            scales = jnp.exp2(exponents) * (1.0 / TOP)
            for at in range(0, rows, BLOCK):
                values = quad[near_slot, at : at + BLOCK, :].astype(jnp.int32).astype(jnp.float32)
                for low in range(0, BLOCK, SHARED):
                    i = (at + low) // SHARED
                    block = pl.ds(at + low, SHARED)
                    median = values[low : low + SHARED] * scales[i : i + 1]
                    moved = MOMENTUM_RATE * held[slot, 0, block, :] + median
                    held[slot, 0, block, :] = moved
                    held[slot, 1, block, :] = held[slot, 1, block, :] + SERVER_RATE * moved
            for i in range(2):
                store(part, near_slot, i).start()
            return carry

        lax.fori_loop(0, SIDE, work, 0)
    for part in range(len(parts)):
        each(part, lambda *at: store(*at).wait())


def update(parts, me, quads, momentum, weights, made=()):
    pieces, rows, _ = momentum.shape
    vmem, hbm = pl.BlockSpec(memory_space=pltpu.VMEM), pl.BlockSpec(memory_space=pltpu.HBM)
    shape = pltpu.HBM(momentum.shape, momentum.dtype)
    in_hbm = [pltpu.with_memory_space_constraint(array, pltpu.HBM) for array in (momentum, weights, *made)]
    slots = SIDE * len(parts)
    return pl.pallas_call(
        lambda *refs: update_kernel(parts, *refs),
        in_specs=[pl.BlockSpec(memory_space=pltpu.SMEM)] + [vmem] * len(quads) + [hbm] * len(in_hbm),
        out_specs=(hbm, hbm),
        out_shape=(shape, shape),
        scratch_shapes=[
            pltpu.VMEM((slots, 2, rows, LANES), jnp.float32),
            pltpu.SemaphoreType.DMA((slots, 2)),
            pltpu.SemaphoreType.DMA((slots, 2)),
        ],
        input_output_aliases={1 + len(quads) + 2 + i: i for i in range(len(made))},
        compiler_params=params(),
        cost_estimate=pl.CostEstimate(flops=1, bytes_accessed=1, transcendentals=0),
    )(me, *quads, *in_hbm)


def along(step, shift):
    pairs = []
    for x in range(SIDE):
        for z in range(SIDE):
            for core in range(2):
                if (core == 0) == (step == 0):
                    to_x, to_z = x, (z + shift) % SIDE
                else:
                    to_x, to_z = (x + shift) % SIDE, z
                pairs.append(((x * SIDE + z) * 2 + core, (to_x * SIDE + to_z) * 2 + core))
    return pairs


def direct(x, counts):
    share = counts / jnp.sum(counts)
    wide = x.astype(jnp.float32)

    def weighted(coefficients):
        return jnp.sum(coefficients[:, None, None] * wide, axis=0)

    median = weighted(share)
    for sweep in range(ITERS):
        squared = lax.psum(jnp.sum(jnp.square(wide - median[None]), axis=(1, 2)), ("wide", "narrow"))
        beta = share / jnp.sqrt(squared + NU_SQUARE)
        median = weighted(beta) / jnp.sum(beta)
    copies = jnp.broadcast_to(median[None], x.shape)
    return lax.all_to_all(copies, "wide", split_axis=0, concat_axis=0, tiled=True)


def shards(deltas, sample_counts, momentum, weights):
    clients = sample_counts.shape[0]
    counts = sample_counts.astype(jnp.float32)
    padded = jnp.pad(counts, (0, LANES - clients)).reshape(1, LANES)
    me = lax.axis_index("wide").astype(jnp.int32).reshape(1)
    x = lax.all_to_all(pack(deltas, clients), "wide", split_axis=0, concat_axis=0, tiled=True)
    devices = lax.axis_size(("wide", "narrow"))
    grams = lax.all_to_all(gram_copies(x, devices), ("wide", "narrow"), split_axis=0, concat_axis=0, tiled=True)
    flat = momentum.shape
    blocks = (clients, momentum.shape[0] // clients // LANES, LANES)
    momentum, weights = momentum.reshape(blocks), weights.reshape(blocks)
    piece, safe = median_of(grams, padded, x)

    near = [piece] + [lax.ppermute(piece, "wide", along(0, shift)) for shift in range(1, SIDE)]
    own = jnp.stack(near)
    ours = [own] + [lax.ppermute(own, "wide", along(1, shift)) for shift in range(1, SIDE)]
    across = [(i, i ^ 1) for i in range(2 * SIDE * SIDE)]
    theirs = lax.ppermute(own, "wide", across)
    first, second = (lax.ppermute(own, "wide", along(1, shift)) for shift in (1, 3))
    made = update([(0, 0), (1, 0)], me, [own, theirs], momentum, weights)
    again_own, *made = lax.optimization_barrier((own, *made))
    last = lax.ppermute(again_own, "wide", along(1, 2))
    first, second, *made = lax.optimization_barrier((first, second, *made))
    theirs = [lax.ppermute(quad, "wide", across) for quad in (first, second)]
    made = update([(0, 1), (0, 3)], me, [first, second], momentum, weights, made)
    last, *made = lax.optimization_barrier((last, *made))
    theirs = theirs + [lax.ppermute(last, "wide", across)]
    made = update([(1, 1), (1, 3)], me, theirs[:2], momentum, weights, made)
    new_momentum, new_weights = update([(0, 2), (1, 2)], me, [last, theirs[2]], momentum, weights, made)

    def again(state):
        new_momentum = MOMENTUM_RATE * momentum + direct(x, counts)
        return jnp.int32(1), new_momentum, weights + SERVER_RATE * new_momentum

    state = (safe[0], new_momentum, new_weights)
    _, new_momentum, new_weights = lax.while_loop(lambda state: state[0] == 0, again, state)
    return (new_weights.reshape(flat), new_momentum.reshape(flat))


def solution(mesh):
    placed = (P("wide", "narrow"), P(), P("narrow"), P("narrow"))
    return jax.shard_map(
        shards, mesh=mesh, in_specs=placed, out_specs=(P("narrow"), P("narrow")), check_vma=False
    )
```

```python
import jax
import jax.numpy as jnp
from jax import lax
from jax.experimental import pallas as pl
from jax.experimental.pallas import tpu as pltpu
from jax.sharding import PartitionSpec as P

ITERS = 3


NU_SQUARE = 1.0
MOMENTUM_RATE = 0.9
SERVER_RATE = 1.0

LANES = 128
GROUP = 16
GRAM_ROWS = 8
BLOCK = 48
SHARED = 24
TOP = 32000.0
SMALLEST = 2.0**-100
SAFE_SHARE = 1.0 / 256.0
VMEM = 24 << 20
SIDE = 4


def params(**more):
    return pltpu.CompilerParams(vmem_limit_bytes=VMEM, **more)


def pack_kernel(flat_ref, packed_ref):
    packed_ref[...] = flat_ref[...].reshape(packed_ref.shape)


def pack(deltas, clients):
    entries = deltas.shape[1]
    rows = entries // LANES
    steps = 2
    packed = pl.pallas_call(
        pack_kernel,
        grid=(steps,),
        in_specs=[pl.BlockSpec((1, entries // steps), lambda i: (0, i))],
        out_specs=pl.BlockSpec((rows // steps, LANES), lambda i: (i, 0)),
        out_shape=jax.ShapeDtypeStruct((rows, LANES), deltas.dtype),
        compiler_params=params(),
    )(deltas)
    return packed.reshape(clients, rows // clients, LANES)


def gram_kernel(x_ref, out_ref):
    clients, rows, _ = x_ref.shape
    wide = clients * GRAM_ROWS
    y = jnp.concatenate(
        [x_ref[:, pl.ds(GRAM_ROWS * k, GRAM_ROWS), :].reshape(wide, LANES) for k in range(rows // GRAM_ROWS)], axis=1
    )
    products = lax.dot_general(y, y, (((1,), (1,)), ((), ())), preferred_element_type=jnp.float32)
    row = lax.broadcasted_iota(jnp.int32, products.shape, 0)
    column = lax.broadcasted_iota(jnp.int32, products.shape, 1)
    products = jnp.where((row & (GRAM_ROWS - 1)) == (column & (GRAM_ROWS - 1)), products, 0.0)
    summed = products.reshape(clients, GRAM_ROWS, wide).sum(axis=1)
    owner = lax.broadcasted_iota(jnp.int32, (wide, LANES), 0) // GRAM_ROWS
    lane = lax.broadcasted_iota(jnp.int32, (wide, LANES), 1)
    place = jnp.where((lane & (clients - 1)) == owner, 1.0, 0.0)
    gram = jnp.dot(summed, place, precision=lax.Precision.HIGHEST, preferred_element_type=jnp.float32)
    row = lax.broadcasted_iota(jnp.int32, gram.shape, 0)
    lane = lax.broadcasted_iota(jnp.int32, gram.shape, 1)
    for j in range(out_ref.shape[1]):
        other = (lane - (4 * j + lane // clients)) & (clients - 1)
        diagonals = jnp.where(row == other, gram, 0.0).sum(axis=0, keepdims=True)
        out_ref[:, j] = jnp.broadcast_to(diagonals[None], (out_ref.shape[0], 1, LANES))


def gram_copies(x, copies):
    clients, rows, _ = x.shape
    return pl.pallas_call(
        gram_kernel,
        out_shape=jax.ShapeDtypeStruct((copies, clients // 8 + 1, 1, LANES), jnp.float32),
        compiler_params=params(),
    )(x)


def encode(total):
    values, exponents = [], []
    for at in range(0, BLOCK, SHARED):
        part = total[at : at + SHARED]
        largest = jnp.maximum(jnp.abs(part).max(axis=0, keepdims=True), SMALLEST)
        exponent = jnp.ceil(jnp.log2(largest))
        values.append(jnp.round(part * (TOP * jnp.exp2(-exponent))))
        exponents.append(exponent)
    return jnp.concatenate(values, axis=0).astype(jnp.int32).astype(jnp.int16), exponents


def encode_into(piece_ref, exponent_ref, rows, total_of):
    exponent_ref[...] = jnp.zeros_like(exponent_ref)

    def step(k, carry):
        at = pl.ds(pl.multiple_of(k * BLOCK, BLOCK), BLOCK)
        values, exponents = encode(total_of(at))
        piece_ref[at, :] = values
        for i, exponent in enumerate(exponents):
            exponent_ref[pl.ds(len(exponents) * k + i, 1), :] = exponent
        return carry

    lax.fori_loop(0, rows // BLOCK, step, 0)
    piece_ref[rows : rows + GROUP, :] = exponent_ref[...].astype(jnp.int32).astype(jnp.int16)


def median_kernel(grams_ref, counts_ref, x_ref, piece_ref, safe_ref, beta_ref, exponent_ref):
    clients, rows, _ = x_ref.shape
    summed = jnp.sum(grams_ref[...], axis=0)
    lane = lax.broadcasted_iota(jnp.int32, (clients, LANES), 1)
    row = lax.broadcasted_iota(jnp.int32, (clients, LANES), 0)
    behind = jnp.where(lane < clients, (lane - row) & (clients - 1), clients)
    half = jnp.zeros((clients, LANES), jnp.float32)
    for k in range(clients // 2 + 1):
        diagonal = summed[k // 4]
        if k % 4:
            diagonal = pltpu.roll(diagonal, LANES - clients * (k % 4), 1)
        half = jnp.where(behind == k, diagonal, half)
    identity = jnp.where(lane == row, 1.0, 0.0)
    turned = lax.dot_general(
        half,
        identity,
        (((0,), (0,)), ((), ())),
        precision=lax.Precision.HIGHEST,
        preferred_element_type=jnp.float32,
    )[:clients]
    gram = jnp.where(behind <= clients // 2, half, turned)
    gram = jnp.where(lane < clients, gram, 0.0)
    square = jnp.where(lane == row, gram, 0.0).sum(axis=0, keepdims=True)
    norm = jnp.sqrt(square)

    square_column = jnp.where(lane == row, gram, 0.0).sum(axis=1, keepdims=True)
    counts = counts_ref[...]
    beta, beta_column = counts, jnp.where(lane == row, counts, 0.0).sum(axis=1, keepdims=True)
    share, share_column = beta, beta_column
    safe = jnp.ones((1, 1), jnp.float32)
    for sweep in range(ITERS):
        part = 1.0 / beta.sum(axis=1, keepdims=True)
        inner = (gram * beta_column).sum(axis=0, keepdims=True)
        inner_column = (gram * beta).sum(axis=1, keepdims=True)
        median_square = (inner * beta).sum(axis=1, keepdims=True) * (part * part)
        mean_norm = (norm * beta).sum(axis=1, keepdims=True) * part
        distance = square - (2.0 * part) * inner + median_square + NU_SQUARE
        distance_column = square_column - (2.0 * part) * inner_column + median_square + NU_SQUARE
        scale = norm + mean_norm
        margin = jnp.where(lane[:1] < clients, distance - SAFE_SHARE * (scale * scale), 1.0)
        safe = jnp.minimum(safe, margin.min(axis=1, keepdims=True))
        beta = share / jnp.sqrt(jnp.maximum(distance, NU_SQUARE))
        beta_column = share_column / jnp.sqrt(jnp.maximum(distance_column, NU_SQUARE))
    beta_column = beta_column / beta.sum(axis=1, keepdims=True)
    safe_ref[0] = jnp.where(safe[0, 0] > 0.0, 1, 0)
    beta_ref[...] = jnp.broadcast_to(beta_column, beta_ref.shape)

    def total_of(at):
        total = jnp.zeros((BLOCK, LANES), jnp.float32)
        for c in range(clients):
            total = total + beta_ref[c : c + 1, :] * x_ref[c, at, :].astype(jnp.float32)
        return total

    encode_into(piece_ref, exponent_ref, rows, total_of)


def median_of(grams, counts, x):
    clients, rows, _ = x.shape
    return pl.pallas_call(
        median_kernel,
        out_shape=(
            jax.ShapeDtypeStruct((rows + GROUP, LANES), jnp.int16),
            jax.ShapeDtypeStruct((1,), jnp.int32),
        ),
        out_specs=(pl.BlockSpec(memory_space=pltpu.VMEM), pl.BlockSpec(memory_space=pltpu.SMEM)),
        scratch_shapes=[pltpu.VMEM((clients, LANES), jnp.float32), pltpu.VMEM((GROUP, LANES), jnp.float32)],
        compiler_params=params(),
    )(grams, counts, x)


def update_kernel(parts, ahead, given, first, me_ref, *refs):
    quads, refs = refs[: len(parts)], refs[len(parts) :]
    (momentum_ref, weights_ref), refs = refs[:2], refs[2:]
    given_ref = refs[2] if given else None
    if ahead:
        new_momentum_ref, new_weights_ref, next_ref, held, in_sem, out_sem, next_sem = refs[-7:]
    else:
        new_momentum_ref, new_weights_ref, held, in_sem, out_sem = refs[-5:]
    rows = momentum_ref.shape[1]
    me = me_ref[0]
    x, z = me // (2 * SIDE), (me // 2) % SIDE

    def place(part, near_slot):
        flip, far_slot = part
        core = (me + flip) % 2
        near = jnp.where(core == 1, z, x)
        far = jnp.where(core == 1, x, z)
        near_at = (near + SIDE - near_slot) % SIDE
        far_at = (far + SIDE - far_slot) % SIDE
        return jnp.where(core == 1, far_at * SIDE + near_at, near_at * SIDE + far_at) * 2 + core

    def copies(group, to_ref, sem):
        def fetch(k, near_slot, i):
            slot = SIDE * k + near_slot
            source = (momentum_ref, weights_ref)[i]
            return pltpu.make_async_copy(source.at[place(group[k], near_slot)], to_ref.at[slot, i], sem.at[slot, i])

        return fetch

    def store(k, near_slot, i):
        slot = SIDE * k + near_slot
        target = (new_momentum_ref, new_weights_ref)[i]
        return pltpu.make_async_copy(held.at[slot, i], target.at[place(parts[k], near_slot)], out_sem.at[slot, i])

    def each(k, act):
        def step(near_slot, carry):
            for i in range(2):
                act(k, near_slot, i)
            return carry

        lax.fori_loop(0, SIDE, step, 0)

    fetch = copies(parts, held, in_sem)
    if not given:
        for k in range(len(parts)):
            each(k, lambda *at: fetch(*at).start())
    if ahead:
        fetch_next = copies(ahead, next_ref, next_sem)
        for k in range(len(ahead)):
            each(k, lambda *at: fetch_next(*at).start())
    source_ref, first = (given_ref, SIDE * first) if given else (held, 0)
    for k in range(len(parts)):
        quad = quads[k]

        def work(near_slot, carry):
            slot = SIDE * k + near_slot
            if not given:
                for i in range(2):
                    fetch(k, near_slot, i).wait()
            exponents = quad[near_slot, rows : rows + GROUP, :].astype(jnp.int32).astype(jnp.float32)
            scales = jnp.exp2(exponents) * (1.0 / TOP)
            for at in range(0, rows, BLOCK):
                values = quad[near_slot, at : at + BLOCK, :].astype(jnp.int32).astype(jnp.float32)
                for low in range(0, BLOCK, SHARED):
                    i = (at + low) // SHARED
                    block = pl.ds(at + low, SHARED)
                    median = values[low : low + SHARED] * scales[i : i + 1]
                    moved = MOMENTUM_RATE * source_ref[first + slot, 0, block, :] + median
                    held[slot, 0, block, :] = moved
                    held[slot, 1, block, :] = source_ref[first + slot, 1, block, :] + SERVER_RATE * moved
            for i in range(2):
                store(k, near_slot, i).start()
            return carry

        lax.fori_loop(0, SIDE, work, 0)
    if ahead:
        for k in range(len(ahead)):
            each(k, lambda *at: fetch_next(*at).wait())
    for k in range(len(parts)):
        each(k, lambda *at: store(*at).wait())


def update(parts, me, quads, momentum, weights, made=(), ahead=(), given=None, first=0):
    pieces, rows, _ = momentum.shape
    vmem, hbm = pl.BlockSpec(memory_space=pltpu.VMEM), pl.BlockSpec(memory_space=pltpu.HBM)
    shape = pltpu.HBM(momentum.shape, momentum.dtype)
    in_hbm = [pltpu.with_memory_space_constraint(array, pltpu.HBM) for array in (momentum, weights, *made)]
    in_vmem = [] if given is None else [pltpu.with_memory_space_constraint(given, pltpu.VMEM)]
    slots, next_slots = SIDE * len(parts), SIDE * len(ahead)
    pair = (2, rows, LANES)
    sems = pltpu.SemaphoreType.DMA((slots, 2))
    more = bool(ahead)
    return pl.pallas_call(
        lambda *refs: update_kernel(parts, ahead, given is not None, first, *refs),
        in_specs=[pl.BlockSpec(memory_space=pltpu.SMEM)] + [vmem] * len(quads) + [hbm] * 2 + [hbm] * len(made)
        + [vmem] * len(in_vmem),
        out_specs=(hbm, hbm) + (vmem,) * more,
        out_shape=(shape, shape) + (pltpu.VMEM((next_slots, *pair), jnp.float32),) * more,
        scratch_shapes=[pltpu.VMEM((slots, *pair), jnp.float32), sems, sems]
        + [pltpu.SemaphoreType.DMA((next_slots, 2))] * more,
        input_output_aliases={1 + len(quads) + 2 + i: i for i in range(len(made))},
        compiler_params=params(),
        cost_estimate=pl.CostEstimate(flops=1, bytes_accessed=1, transcendentals=0),
    )(me, *quads, *in_hbm, *in_vmem)


def along(step, shift):
    pairs = []
    for x in range(SIDE):
        for z in range(SIDE):
            for core in range(2):
                if (core == 1) == (step == 0):
                    to_x, to_z = x, (z + shift) % SIDE
                else:
                    to_x, to_z = (x + shift) % SIDE, z
                pairs.append(((x * SIDE + z) * 2 + core, (to_x * SIDE + to_z) * 2 + core))
    return pairs


def direct(x, counts):
    share = counts / jnp.sum(counts)
    wide = x.astype(jnp.float32)

    def weighted(coefficients):
        return jnp.sum(coefficients[:, None, None] * wide, axis=0)

    median = weighted(share)
    for sweep in range(ITERS):
        squared = lax.psum(jnp.sum(jnp.square(wide - median[None]), axis=(1, 2)), ("wide", "narrow"))
        beta = share / jnp.sqrt(squared + NU_SQUARE)
        median = weighted(beta) / jnp.sum(beta)
    copies = jnp.broadcast_to(median[None], x.shape)
    return lax.all_to_all(copies, "wide", split_axis=0, concat_axis=0, tiled=True)


def shards(deltas, sample_counts, momentum, weights):
    clients = sample_counts.shape[0]
    counts = sample_counts.astype(jnp.float32)
    padded = jnp.pad(counts, (0, LANES - clients)).reshape(1, LANES)
    me = lax.axis_index("wide").astype(jnp.int32).reshape(1)
    x = lax.all_to_all(pack(deltas, clients), "wide", split_axis=0, concat_axis=0, tiled=True)
    devices = lax.axis_size(("wide", "narrow"))
    grams = lax.all_to_all(gram_copies(x, devices), ("wide", "narrow"), split_axis=0, concat_axis=0, tiled=True)
    flat = momentum.shape
    blocks = (clients, momentum.shape[0] // clients // LANES, LANES)
    momentum, weights = momentum.reshape(blocks), weights.reshape(blocks)
    piece, safe = median_of(grams, padded, x)

    near = [piece] + [lax.ppermute(piece, "wide", along(0, shift)) for shift in range(1, SIDE)]
    own = jnp.stack(near)
    ours = [own] + [lax.ppermute(own, "wide", along(1, shift)) for shift in range(1, SIDE)]
    across = [(i, i ^ 1) for i in range(2 * SIDE * SIDE)]
    theirs = lax.ppermute(own, "wide", across)
    first, second = (lax.ppermute(own, "wide", along(1, shift)) for shift in (1, 3))
    made = update([(0, 0), (1, 0)], me, [own, theirs], momentum, weights)
    again_own, *made = lax.optimization_barrier((own, *made))
    last = lax.ppermute(again_own, "wide", along(1, 2))
    first, second, *made = lax.optimization_barrier((first, second, *made))
    theirs = [lax.ppermute(quad, "wide", across) for quad in (first, second)]
    rest = [(1, 1), (1, 3), (0, 2), (1, 2)]
    *made, given = update([(0, 1), (0, 3)], me, [first, second], momentum, weights, made, ahead=rest)
    last, *made = lax.optimization_barrier((last, *made))
    theirs = theirs + [lax.ppermute(last, "wide", across)]
    made = update(rest[:2], me, theirs[:2], momentum, weights, made, given=given)
    new_momentum, new_weights = update(rest[2:], me, [last, theirs[2]], momentum, weights, made, given=given, first=2)

    def again(state):
        new_momentum = MOMENTUM_RATE * momentum + direct(x, counts)
        return jnp.int32(1), new_momentum, weights + SERVER_RATE * new_momentum

    state = (safe[0], new_momentum, new_weights)
    _, new_momentum, new_weights = lax.while_loop(lambda state: state[0] == 0, again, state)
    return (new_weights.reshape(flat), new_momentum.reshape(flat))


def solution(mesh):
    placed = (P("wide", "narrow"), P(), P("narrow"), P("narrow"))
    return jax.shard_map(
        shards, mesh=mesh, in_specs=placed, out_specs=(P("narrow"), P("narrow")), check_vma=False
    )
```

```python
import jax
import jax.numpy as jnp
from jax import lax
from jax.experimental import pallas as pl
from jax.experimental.pallas import tpu as pltpu
from jax.sharding import PartitionSpec as P

ITERS = 3


NU_SQUARE = 1.0
MOMENTUM_RATE = 0.9
SERVER_RATE = 1.0

LANES = 128
GROUP = 16
GRAM_ROWS = 8
BLOCK = 48
SHARED = 24
TOP = 32000.0
SMALLEST = 2.0**-100
SAFE_SHARE = 1.0 / 256.0
VMEM = 24 << 20
SIDE = 4


def params(**more):
    return pltpu.CompilerParams(vmem_limit_bytes=VMEM, **more)


def pack_kernel(flat_ref, packed_ref):
    packed_ref[...] = flat_ref[...].reshape(packed_ref.shape)


def pack(deltas, clients):
    entries = deltas.shape[1]
    rows = entries // LANES
    steps = 2
    packed = pl.pallas_call(
        pack_kernel,
        grid=(steps,),
        in_specs=[pl.BlockSpec((1, entries // steps), lambda i: (0, i))],
        out_specs=pl.BlockSpec((rows // steps, LANES), lambda i: (i, 0)),
        out_shape=jax.ShapeDtypeStruct((rows, LANES), deltas.dtype),
        compiler_params=params(),
    )(deltas)
    return packed.reshape(clients, rows // clients, LANES)


def gram_kernel(x_ref, out_ref):
    clients, rows, _ = x_ref.shape
    wide = clients * GRAM_ROWS
    y = jnp.concatenate(
        [x_ref[:, pl.ds(GRAM_ROWS * k, GRAM_ROWS), :].reshape(wide, LANES) for k in range(rows // GRAM_ROWS)], axis=1
    )
    products = lax.dot_general(y, y, (((1,), (1,)), ((), ())), preferred_element_type=jnp.float32)
    row = lax.broadcasted_iota(jnp.int32, products.shape, 0)
    column = lax.broadcasted_iota(jnp.int32, products.shape, 1)
    products = jnp.where((row & (GRAM_ROWS - 1)) == (column & (GRAM_ROWS - 1)), products, 0.0)
    summed = products.reshape(clients, GRAM_ROWS, wide).sum(axis=1)
    owner = lax.broadcasted_iota(jnp.int32, (wide, LANES), 0) // GRAM_ROWS
    lane = lax.broadcasted_iota(jnp.int32, (wide, LANES), 1)
    place = jnp.where((lane & (clients - 1)) == owner, 1.0, 0.0)
    gram = jnp.dot(summed, place, precision=lax.Precision.HIGHEST, preferred_element_type=jnp.float32)
    row = lax.broadcasted_iota(jnp.int32, gram.shape, 0)
    lane = lax.broadcasted_iota(jnp.int32, gram.shape, 1)
    for j in range(out_ref.shape[1]):
        other = (lane - (4 * j + lane // clients)) & (clients - 1)
        diagonals = jnp.where(row == other, gram, 0.0).sum(axis=0, keepdims=True)
        out_ref[:, j] = jnp.broadcast_to(diagonals[None], (out_ref.shape[0], 1, LANES))


def gram_copies(x, copies):
    clients, rows, _ = x.shape
    return pl.pallas_call(
        gram_kernel,
        out_shape=jax.ShapeDtypeStruct((copies, clients // 8 + 1, 1, LANES), jnp.float32),
        compiler_params=params(),
    )(x)


def encode(total):
    values, exponents = [], []
    for at in range(0, BLOCK, SHARED):
        part = total[at : at + SHARED]
        largest = jnp.maximum(jnp.abs(part).max(axis=0, keepdims=True), SMALLEST)
        exponent = jnp.ceil(jnp.log2(largest))
        values.append(jnp.round(part * (TOP * jnp.exp2(-exponent))))
        exponents.append(exponent)
    return jnp.concatenate(values, axis=0).astype(jnp.int32).astype(jnp.int16), exponents


def encode_into(piece_ref, exponent_ref, rows, total_of):
    exponent_ref[...] = jnp.zeros_like(exponent_ref)

    def step(k, carry):
        at = pl.ds(pl.multiple_of(k * BLOCK, BLOCK), BLOCK)
        values, exponents = encode(total_of(at))
        piece_ref[at, :] = values
        for i, exponent in enumerate(exponents):
            exponent_ref[pl.ds(len(exponents) * k + i, 1), :] = exponent
        return carry

    lax.fori_loop(0, rows // BLOCK, step, 0)
    piece_ref[rows : rows + GROUP, :] = exponent_ref[...].astype(jnp.int32).astype(jnp.int16)


def median_kernel(grams_ref, counts_ref, x_ref, piece_ref, safe_ref, beta_ref, exponent_ref):
    clients, rows, _ = x_ref.shape
    summed = jnp.sum(grams_ref[...], axis=0)
    lane = lax.broadcasted_iota(jnp.int32, (clients, LANES), 1)
    row = lax.broadcasted_iota(jnp.int32, (clients, LANES), 0)
    behind = jnp.where(lane < clients, (lane - row) & (clients - 1), clients)
    half = jnp.zeros((clients, LANES), jnp.float32)
    for k in range(clients // 2 + 1):
        diagonal = summed[k // 4]
        if k % 4:
            diagonal = pltpu.roll(diagonal, LANES - clients * (k % 4), 1)
        half = jnp.where(behind == k, diagonal, half)
    identity = jnp.where(lane == row, 1.0, 0.0)
    turned = lax.dot_general(
        half,
        identity,
        (((0,), (0,)), ((), ())),
        precision=lax.Precision.HIGHEST,
        preferred_element_type=jnp.float32,
    )[:clients]
    gram = jnp.where(behind <= clients // 2, half, turned)
    gram = jnp.where(lane < clients, gram, 0.0)
    square = jnp.where(lane == row, gram, 0.0).sum(axis=0, keepdims=True)
    norm = jnp.sqrt(square)

    square_column = jnp.where(lane == row, gram, 0.0).sum(axis=1, keepdims=True)
    counts = counts_ref[...]
    beta, beta_column = counts, jnp.where(lane == row, counts, 0.0).sum(axis=1, keepdims=True)
    share, share_column = beta, beta_column
    safe = jnp.ones((1, 1), jnp.float32)
    for sweep in range(ITERS):
        part = 1.0 / beta.sum(axis=1, keepdims=True)
        inner = (gram * beta_column).sum(axis=0, keepdims=True)
        inner_column = (gram * beta).sum(axis=1, keepdims=True)
        median_square = (inner * beta).sum(axis=1, keepdims=True) * (part * part)
        mean_norm = (norm * beta).sum(axis=1, keepdims=True) * part
        distance = square - (2.0 * part) * inner + median_square + NU_SQUARE
        distance_column = square_column - (2.0 * part) * inner_column + median_square + NU_SQUARE
        scale = norm + mean_norm
        margin = jnp.where(lane[:1] < clients, distance - SAFE_SHARE * (scale * scale), 1.0)
        safe = jnp.minimum(safe, margin.min(axis=1, keepdims=True))
        beta = share / jnp.sqrt(jnp.maximum(distance, NU_SQUARE))
        beta_column = share_column / jnp.sqrt(jnp.maximum(distance_column, NU_SQUARE))
    beta_column = beta_column / beta.sum(axis=1, keepdims=True)
    safe_ref[0] = jnp.where(safe[0, 0] > 0.0, 1, 0)
    beta_ref[...] = jnp.broadcast_to(beta_column, beta_ref.shape)

    def total_of(at):
        total = jnp.zeros((BLOCK, LANES), jnp.float32)
        for c in range(clients):
            total = total + beta_ref[c : c + 1, :] * x_ref[c, at, :].astype(jnp.float32)
        return total

    encode_into(piece_ref, exponent_ref, rows, total_of)


def median_of(grams, counts, x):
    clients, rows, _ = x.shape
    return pl.pallas_call(
        median_kernel,
        out_shape=(
            jax.ShapeDtypeStruct((rows + GROUP, LANES), jnp.int16),
            jax.ShapeDtypeStruct((1,), jnp.int32),
        ),
        out_specs=(pl.BlockSpec(memory_space=pltpu.VMEM), pl.BlockSpec(memory_space=pltpu.SMEM)),
        scratch_shapes=[pltpu.VMEM((clients, LANES), jnp.float32), pltpu.VMEM((GROUP, LANES), jnp.float32)],
        compiler_params=params(),
    )(grams, counts, x)


def update_kernel(parts, ahead, given, first, me_ref, *refs):
    quads, refs = refs[: len(parts)], refs[len(parts) :]
    (momentum_ref, weights_ref), refs = refs[:2], refs[2:]
    given_ref = refs[2] if given else None
    if ahead:
        new_momentum_ref, new_weights_ref, next_ref, held, in_sem, out_sem, next_sem = refs[-7:]
    else:
        new_momentum_ref, new_weights_ref, held, in_sem, out_sem = refs[-5:]
    rows = momentum_ref.shape[1]
    me = me_ref[0]
    x, z = me // (2 * SIDE), (me // 2) % SIDE

    def place(part, near_slot):
        flip, far_slot = part
        core = (me + flip) % 2
        near = jnp.where(core == 1, z, x)
        far = jnp.where(core == 1, x, z)
        near_at = (near + SIDE - near_slot) % SIDE
        far_at = (far + SIDE - far_slot) % SIDE
        return jnp.where(core == 1, far_at * SIDE + near_at, near_at * SIDE + far_at) * 2 + core

    def copies(group, to_ref, sem):
        def fetch(k, near_slot, i):
            slot = SIDE * k + near_slot
            source = (momentum_ref, weights_ref)[i]
            return pltpu.make_async_copy(source.at[place(group[k], near_slot)], to_ref.at[slot, i], sem.at[slot, i])

        return fetch

    def store(k, near_slot, i):
        slot = SIDE * k + near_slot
        target = (new_momentum_ref, new_weights_ref)[i]
        return pltpu.make_async_copy(held.at[slot, i], target.at[place(parts[k], near_slot)], out_sem.at[slot, i])

    def each(k, act):
        def step(near_slot, carry):
            for i in range(2):
                act(k, near_slot, i)
            return carry

        lax.fori_loop(0, SIDE, step, 0)

    fetch = copies(parts, held, in_sem)
    if not given:
        for k in range(len(parts)):
            each(k, lambda *at: fetch(*at).start())
    if ahead:
        fetch_next = copies(ahead, next_ref, next_sem)
        for k in range(len(ahead)):
            each(k, lambda *at: fetch_next(*at).start())
    source_ref, first = (given_ref, SIDE * first) if given else (held, 0)
    for k in range(len(parts)):
        quad = quads[k]

        def work(near_slot, carry):
            slot = SIDE * k + near_slot
            if not given:
                for i in range(2):
                    fetch(k, near_slot, i).wait()
            exponents = quad[near_slot, rows : rows + GROUP, :].astype(jnp.int32).astype(jnp.float32)
            scales = jnp.exp2(exponents) * (1.0 / TOP)
            for at in range(0, rows, BLOCK):
                values = quad[near_slot, at : at + BLOCK, :].astype(jnp.int32).astype(jnp.float32)
                for low in range(0, BLOCK, SHARED):
                    i = (at + low) // SHARED
                    block = pl.ds(at + low, SHARED)
                    median = values[low : low + SHARED] * scales[i : i + 1]
                    moved = MOMENTUM_RATE * source_ref[first + slot, 0, block, :] + median
                    held[slot, 0, block, :] = moved
                    held[slot, 1, block, :] = source_ref[first + slot, 1, block, :] + SERVER_RATE * moved
            for i in range(2):
                store(k, near_slot, i).start()
            return carry

        lax.fori_loop(0, SIDE, work, 0)
    if ahead:
        for k in range(len(ahead)):
            each(k, lambda *at: fetch_next(*at).wait())
    for k in range(len(parts)):
        each(k, lambda *at: store(*at).wait())


def update(parts, me, quads, momentum, weights, made=(), ahead=(), given=None, first=0):
    pieces, rows, _ = momentum.shape
    vmem, hbm = pl.BlockSpec(memory_space=pltpu.VMEM), pl.BlockSpec(memory_space=pltpu.HBM)
    shape = pltpu.HBM(momentum.shape, momentum.dtype)
    in_hbm = [pltpu.with_memory_space_constraint(array, pltpu.HBM) for array in (momentum, weights, *made)]
    in_vmem = [] if given is None else [pltpu.with_memory_space_constraint(given, pltpu.VMEM)]
    slots, next_slots = SIDE * len(parts), SIDE * len(ahead)
    pair = (2, rows, LANES)
    sems = pltpu.SemaphoreType.DMA((slots, 2))
    more = bool(ahead)
    return pl.pallas_call(
        lambda *refs: update_kernel(parts, ahead, given is not None, first, *refs),
        in_specs=[pl.BlockSpec(memory_space=pltpu.SMEM)] + [vmem] * len(quads) + [hbm] * 2 + [hbm] * len(made)
        + [vmem] * len(in_vmem),
        out_specs=(hbm, hbm) + (vmem,) * more,
        out_shape=(shape, shape) + (pltpu.VMEM((next_slots, *pair), jnp.float32),) * more,
        scratch_shapes=[pltpu.VMEM((slots, *pair), jnp.float32), sems, sems]
        + [pltpu.SemaphoreType.DMA((next_slots, 2))] * more,
        input_output_aliases={1 + len(quads) + 2 + i: i for i in range(len(made))},
        compiler_params=params(),
        cost_estimate=pl.CostEstimate(flops=1, bytes_accessed=1, transcendentals=0),
    )(me, *quads, *in_hbm, *in_vmem)


def along(step, shift):
    pairs = []
    for x in range(SIDE):
        for z in range(SIDE):
            for core in range(2):
                if (core == 1) == (step == 0):
                    to_x, to_z = x, (z + shift) % SIDE
                else:
                    to_x, to_z = (x + shift) % SIDE, z
                pairs.append(((x * SIDE + z) * 2 + core, (to_x * SIDE + to_z) * 2 + core))
    return pairs


def direct(x, counts):
    share = counts / jnp.sum(counts)
    wide = x.astype(jnp.float32)

    def weighted(coefficients):
        return jnp.sum(coefficients[:, None, None] * wide, axis=0)

    median = weighted(share)
    for sweep in range(ITERS):
        squared = lax.psum(jnp.sum(jnp.square(wide - median[None]), axis=(1, 2)), ("wide", "narrow"))
        beta = share / jnp.sqrt(squared + NU_SQUARE)
        median = weighted(beta) / jnp.sum(beta)
    copies = jnp.broadcast_to(median[None], x.shape)
    return lax.all_to_all(copies, "wide", split_axis=0, concat_axis=0, tiled=True)


def shards(deltas, sample_counts, momentum, weights):
    clients = sample_counts.shape[0]
    counts = sample_counts.astype(jnp.float32)
    padded = jnp.pad(counts, (0, LANES - clients)).reshape(1, LANES)
    me = lax.axis_index("wide").astype(jnp.int32).reshape(1)
    x = lax.all_to_all(pack(deltas, clients), "wide", split_axis=0, concat_axis=0, tiled=True)
    devices = lax.axis_size(("wide", "narrow"))
    grams = lax.all_to_all(gram_copies(x, devices), ("wide", "narrow"), split_axis=0, concat_axis=0, tiled=True)
    flat = momentum.shape
    blocks = (clients, momentum.shape[0] // clients // LANES, LANES)
    momentum, weights = momentum.reshape(blocks), weights.reshape(blocks)
    piece, safe = median_of(grams, padded, x)

    near = [piece] + [lax.ppermute(piece, "wide", along(0, shift)) for shift in range(1, SIDE)]
    own = jnp.stack(near)
    ours = [own] + [lax.ppermute(own, "wide", along(1, shift)) for shift in range(1, SIDE)]
    across = [(i, i ^ 1) for i in range(2 * SIDE * SIDE)]
    theirs = lax.ppermute(own, "wide", across)
    first, second = (lax.ppermute(own, "wide", along(1, shift)) for shift in (1, 3))
    made = update([(0, 0), (1, 0)], me, [own, theirs], momentum, weights)
    again_own, *made = lax.optimization_barrier((own, *made))
    last = lax.ppermute(again_own, "wide", along(1, 2))
    rest = [(0, 3), (1, 1), (1, 3), (0, 2), (1, 2)]
    first, *made = lax.optimization_barrier((first, *made))
    theirs = [lax.ppermute(first, "wide", across)]
    *made, given = update([(0, 1)], me, [first], momentum, weights, made, ahead=rest)
    second, *made = lax.optimization_barrier((second, *made))
    theirs = theirs + [lax.ppermute(second, "wide", across)]
    made = update(rest[:1], me, [second], momentum, weights, made, given=given)
    last, *made = lax.optimization_barrier((last, *made))
    theirs = theirs + [lax.ppermute(last, "wide", across)]
    made = update(rest[1:3], me, theirs[:2], momentum, weights, made, given=given, first=1)
    new_momentum, new_weights = update(rest[3:], me, [last, theirs[2]], momentum, weights, made, given=given, first=3)

    def again(state):
        new_momentum = MOMENTUM_RATE * momentum + direct(x, counts)
        return jnp.int32(1), new_momentum, weights + SERVER_RATE * new_momentum

    state = (safe[0], new_momentum, new_weights)
    _, new_momentum, new_weights = lax.while_loop(lambda state: state[0] == 0, again, state)
    return (new_weights.reshape(flat), new_momentum.reshape(flat))


def solution(mesh):
    placed = (P("wide", "narrow"), P(), P("narrow"), P("narrow"))
    return jax.shard_map(
        shards, mesh=mesh, in_specs=placed, out_specs=(P("narrow"), P("narrow")), check_vma=False
    )
```

```python
import jax
import jax.numpy as jnp
from jax import lax
from jax.experimental import pallas as pl
from jax.experimental.pallas import tpu as pltpu
from jax.sharding import PartitionSpec as P

ITERS = 3


NU_SQUARE = 1.0
MOMENTUM_RATE = 0.9
SERVER_RATE = 1.0

LANES = 128
GROUP = 16
GRAM_ROWS = 8
BLOCK = 48
SHARED = 24
TOP = 32000.0
SMALLEST = 2.0**-100
SAFE_SHARE = 1.0 / 256.0
VMEM = 24 << 20
SIDE = 4


def params(**more):
    return pltpu.CompilerParams(vmem_limit_bytes=VMEM, **more)


def pack_kernel(flat_ref, packed_ref):
    packed_ref[...] = flat_ref[...].reshape(packed_ref.shape)


def pack(deltas, clients):
    entries = deltas.shape[1]
    rows = entries // LANES
    steps = 2
    packed = pl.pallas_call(
        pack_kernel,
        grid=(steps,),
        in_specs=[pl.BlockSpec((1, entries // steps), lambda i: (0, i))],
        out_specs=pl.BlockSpec((rows // steps, LANES), lambda i: (i, 0)),
        out_shape=jax.ShapeDtypeStruct((rows, LANES), deltas.dtype),
        compiler_params=params(),
    )(deltas)
    return packed.reshape(clients, rows // clients, LANES)


def gram_kernel(x_ref, out_ref):
    clients, rows, _ = x_ref.shape
    wide = clients * GRAM_ROWS
    y = jnp.concatenate(
        [x_ref[:, pl.ds(GRAM_ROWS * k, GRAM_ROWS), :].reshape(wide, LANES) for k in range(rows // GRAM_ROWS)], axis=1
    )
    products = lax.dot_general(y, y, (((1,), (1,)), ((), ())), preferred_element_type=jnp.float32)
    row = lax.broadcasted_iota(jnp.int32, products.shape, 0)
    column = lax.broadcasted_iota(jnp.int32, products.shape, 1)
    products = jnp.where((row & (GRAM_ROWS - 1)) == (column & (GRAM_ROWS - 1)), products, 0.0)
    summed = products.reshape(clients, GRAM_ROWS, wide).sum(axis=1)
    owner = lax.broadcasted_iota(jnp.int32, (wide, LANES), 0) // GRAM_ROWS
    lane = lax.broadcasted_iota(jnp.int32, (wide, LANES), 1)
    place = jnp.where((lane & (clients - 1)) == owner, 1.0, 0.0)
    gram = jnp.dot(summed, place, precision=lax.Precision.HIGHEST, preferred_element_type=jnp.float32)
    row = lax.broadcasted_iota(jnp.int32, gram.shape, 0)
    lane = lax.broadcasted_iota(jnp.int32, gram.shape, 1)
    for j in range(out_ref.shape[1]):
        other = (lane - (4 * j + lane // clients)) & (clients - 1)
        diagonals = jnp.where(row == other, gram, 0.0).sum(axis=0, keepdims=True)
        out_ref[:, j] = jnp.broadcast_to(diagonals[None], (out_ref.shape[0], 1, LANES))


def gram_copies(x, copies):
    clients, rows, _ = x.shape
    return pl.pallas_call(
        gram_kernel,
        out_shape=jax.ShapeDtypeStruct((copies, clients // 8 + 1, 1, LANES), jnp.float32),
        compiler_params=params(),
    )(x)


def encode(total):
    values, exponents = [], []
    for at in range(0, BLOCK, SHARED):
        part = total[at : at + SHARED]
        largest = jnp.maximum(jnp.abs(part).max(axis=0, keepdims=True), SMALLEST)
        exponent = jnp.ceil(jnp.log2(largest))
        values.append(jnp.round(part * (TOP * jnp.exp2(-exponent))))
        exponents.append(exponent)
    return jnp.concatenate(values, axis=0).astype(jnp.int32).astype(jnp.int16), exponents


def encode_into(piece_ref, exponent_ref, rows, total_of):
    exponent_ref[...] = jnp.zeros_like(exponent_ref)

    def step(k, carry):
        at = pl.ds(pl.multiple_of(k * BLOCK, BLOCK), BLOCK)
        values, exponents = encode(total_of(at))
        piece_ref[at, :] = values
        for i, exponent in enumerate(exponents):
            exponent_ref[pl.ds(len(exponents) * k + i, 1), :] = exponent
        return carry

    lax.fori_loop(0, rows // BLOCK, step, 0)
    piece_ref[rows : rows + GROUP, :] = exponent_ref[...].astype(jnp.int32).astype(jnp.int16)


def median_kernel(grams_ref, counts_ref, x_ref, piece_ref, safe_ref, beta_ref, exponent_ref):
    clients, rows, _ = x_ref.shape
    summed = jnp.sum(grams_ref[...], axis=0)
    lane = lax.broadcasted_iota(jnp.int32, (clients, LANES), 1)
    row = lax.broadcasted_iota(jnp.int32, (clients, LANES), 0)
    behind = jnp.where(lane < clients, (lane - row) & (clients - 1), clients)
    half = jnp.zeros((clients, LANES), jnp.float32)
    for k in range(clients // 2 + 1):
        diagonal = summed[k // 4]
        if k % 4:
            diagonal = pltpu.roll(diagonal, LANES - clients * (k % 4), 1)
        half = jnp.where(behind == k, diagonal, half)
    identity = jnp.where(lane == row, 1.0, 0.0)
    turned = lax.dot_general(
        half,
        identity,
        (((0,), (0,)), ((), ())),
        precision=lax.Precision.HIGHEST,
        preferred_element_type=jnp.float32,
    )[:clients]
    gram = jnp.where(behind <= clients // 2, half, turned)
    gram = jnp.where(lane < clients, gram, 0.0)
    square = jnp.where(lane == row, gram, 0.0).sum(axis=0, keepdims=True)
    norm = jnp.sqrt(square)

    square_column = jnp.where(lane == row, gram, 0.0).sum(axis=1, keepdims=True)
    counts = counts_ref[...]
    beta, beta_column = counts, jnp.where(lane == row, counts, 0.0).sum(axis=1, keepdims=True)
    share, share_column = beta, beta_column
    safe = jnp.ones((1, 1), jnp.float32)
    for sweep in range(ITERS):
        part = 1.0 / beta.sum(axis=1, keepdims=True)
        inner = (gram * beta_column).sum(axis=0, keepdims=True)
        inner_column = (gram * beta).sum(axis=1, keepdims=True)
        median_square = (inner * beta).sum(axis=1, keepdims=True) * (part * part)
        mean_norm = (norm * beta).sum(axis=1, keepdims=True) * part
        distance = square - (2.0 * part) * inner + median_square + NU_SQUARE
        distance_column = square_column - (2.0 * part) * inner_column + median_square + NU_SQUARE
        scale = norm + mean_norm
        margin = jnp.where(lane[:1] < clients, distance - SAFE_SHARE * (scale * scale), 1.0)
        safe = jnp.minimum(safe, margin.min(axis=1, keepdims=True))
        beta = share / jnp.sqrt(jnp.maximum(distance, NU_SQUARE))
        beta_column = share_column / jnp.sqrt(jnp.maximum(distance_column, NU_SQUARE))
    beta_column = beta_column / beta.sum(axis=1, keepdims=True)
    safe_ref[0] = jnp.where(safe[0, 0] > 0.0, 1, 0)
    beta_ref[...] = jnp.broadcast_to(beta_column, beta_ref.shape)

    def total_of(at):
        total = jnp.zeros((BLOCK, LANES), jnp.float32)
        for c in range(clients):
            total = total + beta_ref[c : c + 1, :] * x_ref[c, at, :].astype(jnp.float32)
        return total

    encode_into(piece_ref, exponent_ref, rows, total_of)


def median_of(grams, counts, x):
    clients, rows, _ = x.shape
    return pl.pallas_call(
        median_kernel,
        out_shape=(
            jax.ShapeDtypeStruct((rows + GROUP, LANES), jnp.int16),
            jax.ShapeDtypeStruct((1,), jnp.int32),
        ),
        out_specs=(pl.BlockSpec(memory_space=pltpu.VMEM), pl.BlockSpec(memory_space=pltpu.SMEM)),
        scratch_shapes=[pltpu.VMEM((clients, LANES), jnp.float32), pltpu.VMEM((GROUP, LANES), jnp.float32)],
        compiler_params=params(),
    )(grams, counts, x)


def update_kernel(parts, ahead, given, first, me_ref, *refs):
    quads, refs = refs[: len(parts)], refs[len(parts) :]
    (momentum_ref, weights_ref), refs = refs[:2], refs[2:]
    given_ref = refs[2] if given else None
    if ahead:
        new_momentum_ref, new_weights_ref, next_ref, held, in_sem, out_sem, next_sem = refs[-7:]
    else:
        new_momentum_ref, new_weights_ref, held, in_sem, out_sem = refs[-5:]
    rows = momentum_ref.shape[1]
    me = me_ref[0]
    x, z = me // (2 * SIDE), (me // 2) % SIDE

    def place(part, near_slot):
        flip, far_slot = part
        core = (me + flip) % 2
        near = jnp.where(core == 1, z, x)
        far = jnp.where(core == 1, x, z)
        near_at = (near + SIDE - near_slot) % SIDE
        far_at = (far + SIDE - far_slot) % SIDE
        return jnp.where(core == 1, far_at * SIDE + near_at, near_at * SIDE + far_at) * 2 + core

    def copies(group, to_ref, sem):
        def fetch(k, near_slot, i):
            slot = SIDE * k + near_slot
            source = (momentum_ref, weights_ref)[i]
            return pltpu.make_async_copy(source.at[place(group[k], near_slot)], to_ref.at[slot, i], sem.at[slot, i])

        return fetch

    def store(k, near_slot, i):
        slot = SIDE * k + near_slot
        target = (new_momentum_ref, new_weights_ref)[i]
        return pltpu.make_async_copy(held.at[slot, i], target.at[place(parts[k], near_slot)], out_sem.at[slot, i])

    def each(k, act):
        def step(near_slot, carry):
            for i in range(2):
                act(k, near_slot, i)
            return carry

        lax.fori_loop(0, SIDE, step, 0)

    fetch = copies(parts, held, in_sem)
    if not given:
        for k in range(len(parts)):
            each(k, lambda *at: fetch(*at).start())
    if ahead:
        fetch_next = copies(ahead, next_ref, next_sem)
        for k in range(len(ahead)):
            each(k, lambda *at: fetch_next(*at).start())
    source_ref, first = (given_ref, SIDE * first) if given else (held, 0)
    for k in range(len(parts)):
        quad = quads[k]

        def work(near_slot, carry):
            slot = SIDE * k + near_slot
            if not given:
                for i in range(2):
                    fetch(k, near_slot, i).wait()
            exponents = quad[near_slot, rows : rows + GROUP, :].astype(jnp.int32).astype(jnp.float32)
            scales = jnp.exp2(exponents) * (1.0 / TOP)
            for at in range(0, rows, BLOCK):
                values = quad[near_slot, at : at + BLOCK, :].astype(jnp.int32).astype(jnp.float32)
                for low in range(0, BLOCK, SHARED):
                    i = (at + low) // SHARED
                    block = pl.ds(at + low, SHARED)
                    median = values[low : low + SHARED] * scales[i : i + 1]
                    moved = MOMENTUM_RATE * source_ref[first + slot, 0, block, :] + median
                    held[slot, 0, block, :] = moved
                    held[slot, 1, block, :] = source_ref[first + slot, 1, block, :] + SERVER_RATE * moved
            for i in range(2):
                store(k, near_slot, i).start()
            return carry

        lax.fori_loop(0, SIDE, work, 0)
    if ahead:
        for k in range(len(ahead)):
            each(k, lambda *at: fetch_next(*at).wait())
    for k in range(len(parts)):
        each(k, lambda *at: store(*at).wait())


def update(parts, me, quads, momentum, weights, made=(), ahead=(), given=None, first=0):
    pieces, rows, _ = momentum.shape
    vmem, hbm = pl.BlockSpec(memory_space=pltpu.VMEM), pl.BlockSpec(memory_space=pltpu.HBM)
    shape = pltpu.HBM(momentum.shape, momentum.dtype)
    in_hbm = [pltpu.with_memory_space_constraint(array, pltpu.HBM) for array in (momentum, weights, *made)]
    in_vmem = [] if given is None else [pltpu.with_memory_space_constraint(given, pltpu.VMEM)]
    slots, next_slots = SIDE * len(parts), SIDE * len(ahead)
    pair = (2, rows, LANES)
    sems = pltpu.SemaphoreType.DMA((slots, 2))
    more = bool(ahead)
    return pl.pallas_call(
        lambda *refs: update_kernel(parts, ahead, given is not None, first, *refs),
        in_specs=[pl.BlockSpec(memory_space=pltpu.SMEM)] + [vmem] * len(quads) + [hbm] * 2 + [hbm] * len(made)
        + [vmem] * len(in_vmem),
        out_specs=(hbm, hbm) + (vmem,) * more,
        out_shape=(shape, shape) + (pltpu.VMEM((next_slots, *pair), jnp.float32),) * more,
        scratch_shapes=[pltpu.VMEM((slots, *pair), jnp.float32), sems, sems]
        + [pltpu.SemaphoreType.DMA((next_slots, 2))] * more,
        input_output_aliases={1 + len(quads) + 2 + i: i for i in range(len(made))},
        compiler_params=params(),
        cost_estimate=pl.CostEstimate(flops=1, bytes_accessed=1, transcendentals=0),
    )(me, *quads, *in_hbm, *in_vmem)


def along(step, shift):
    pairs = []
    for x in range(SIDE):
        for z in range(SIDE):
            for core in range(2):
                if (core == 1) == (step == 0):
                    to_x, to_z = x, (z + shift) % SIDE
                else:
                    to_x, to_z = (x + shift) % SIDE, z
                pairs.append(((x * SIDE + z) * 2 + core, (to_x * SIDE + to_z) * 2 + core))
    return pairs


def direct(x, counts):
    share = counts / jnp.sum(counts)
    wide = x.astype(jnp.float32)

    def weighted(coefficients):
        return jnp.sum(coefficients[:, None, None] * wide, axis=0)

    median = weighted(share)
    for sweep in range(ITERS):
        squared = lax.psum(jnp.sum(jnp.square(wide - median[None]), axis=(1, 2)), ("wide", "narrow"))
        beta = share / jnp.sqrt(squared + NU_SQUARE)
        median = weighted(beta) / jnp.sum(beta)
    copies = jnp.broadcast_to(median[None], x.shape)
    return lax.all_to_all(copies, "wide", split_axis=0, concat_axis=0, tiled=True)


def shards(deltas, sample_counts, momentum, weights):
    clients = sample_counts.shape[0]
    counts = sample_counts.astype(jnp.float32)
    padded = jnp.pad(counts, (0, LANES - clients)).reshape(1, LANES)
    me = lax.axis_index("wide").astype(jnp.int32).reshape(1)
    x = lax.all_to_all(pack(deltas, clients), "wide", split_axis=0, concat_axis=0, tiled=True)
    devices = lax.axis_size(("wide", "narrow"))
    grams = lax.all_to_all(gram_copies(x, devices), ("wide", "narrow"), split_axis=0, concat_axis=0, tiled=True)
    flat = momentum.shape
    blocks = (clients, momentum.shape[0] // clients // LANES, LANES)
    momentum, weights = momentum.reshape(blocks), weights.reshape(blocks)
    piece, safe = median_of(grams, padded, x)

    near = [piece] + [lax.ppermute(piece, "wide", along(0, shift)) for shift in range(1, SIDE)]
    own = jnp.stack(near)
    ours = [own] + [lax.ppermute(own, "wide", along(1, shift)) for shift in range(1, SIDE)]
    across = [(i, i ^ 1) for i in range(2 * SIDE * SIDE)]
    theirs = lax.ppermute(own, "wide", across)
    first, second = (lax.ppermute(own, "wide", along(1, shift)) for shift in (1, 3))
    sibling = theirs
    made = update([(0, 0)], me, [own], momentum, weights)
    again_own, *made = lax.optimization_barrier((own, *made))
    last = lax.ppermute(again_own, "wide", along(1, 2))
    rest = [(1, 0), (0, 3), (1, 1), (1, 3), (0, 2), (1, 2)]
    first, *made = lax.optimization_barrier((first, *made))
    theirs = [lax.ppermute(first, "wide", across)]
    *made, given = update([(0, 1)], me, [first], momentum, weights, made, ahead=rest)
    second, *made = lax.optimization_barrier((second, *made))
    theirs = theirs + [lax.ppermute(second, "wide", across)]
    made = update(rest[:2], me, [sibling, second], momentum, weights, made, given=given)
    last, *made = lax.optimization_barrier((last, *made))
    theirs = theirs + [lax.ppermute(last, "wide", across)]
    made = update(rest[2:4], me, theirs[:2], momentum, weights, made, given=given, first=2)
    new_momentum, new_weights = update(rest[4:], me, [last, theirs[2]], momentum, weights, made, given=given, first=4)

    def again(state):
        new_momentum = MOMENTUM_RATE * momentum + direct(x, counts)
        return jnp.int32(1), new_momentum, weights + SERVER_RATE * new_momentum

    state = (safe[0], new_momentum, new_weights)
    _, new_momentum, new_weights = lax.while_loop(lambda state: state[0] == 0, again, state)
    return (new_weights.reshape(flat), new_momentum.reshape(flat))


def solution(mesh):
    placed = (P("wide", "narrow"), P(), P("narrow"), P("narrow"))
    return jax.shard_map(
        shards, mesh=mesh, in_specs=placed, out_specs=(P("narrow"), P("narrow")), check_vma=False
    )
```

```python
import jax
import jax.numpy as jnp
from jax import lax
from jax.experimental import pallas as pl
from jax.experimental.pallas import tpu as pltpu
from jax.sharding import PartitionSpec as P

ITERS = 3


NU_SQUARE = 1.0
MOMENTUM_RATE = 0.9
SERVER_RATE = 1.0

LANES = 128
GROUP = 16
GRAM_ROWS = 8
BLOCK = 48
SHARED = 24
TOP = 32000.0
SMALLEST = 2.0**-100
SAFE_SHARE = 1.0 / 256.0
VMEM = 24 << 20
SIDE = 4


def params(**more):
    return pltpu.CompilerParams(vmem_limit_bytes=VMEM, **more)


def pack_kernel(flat_ref, packed_ref, held, sem):
    parts = sem.shape[0]
    entries, rows = flat_ref.shape[1] // parts, packed_ref.shape[0] // parts

    def fetch(i):
        at = pl.ds(i * entries, entries)
        return pltpu.make_async_copy(flat_ref.at[:, at], held.at[:, at], sem.at[i])

    for i in range(parts):
        fetch(i).start()
    for i in range(parts):
        fetch(i).wait()
        packed_ref[i * rows : (i + 1) * rows, :] = held[:, i * entries : (i + 1) * entries].reshape(rows, LANES)


def pack(deltas, clients):
    rows = deltas.shape[1] // LANES
    packed = pl.pallas_call(
        pack_kernel,
        in_specs=[pl.BlockSpec(memory_space=pltpu.HBM)],
        out_specs=pl.BlockSpec(memory_space=pltpu.VMEM),
        out_shape=pltpu.VMEM((rows, LANES), deltas.dtype),
        scratch_shapes=[pltpu.VMEM(deltas.shape, deltas.dtype), pltpu.SemaphoreType.DMA((8,))],
        compiler_params=params(),
    )(pltpu.with_memory_space_constraint(deltas, pltpu.HBM))
    return packed.reshape(clients, rows // clients, LANES)


def gram_kernel(x_ref, out_ref):
    clients, rows, _ = x_ref.shape
    wide = clients * GRAM_ROWS
    y = jnp.concatenate(
        [x_ref[:, pl.ds(GRAM_ROWS * k, GRAM_ROWS), :].reshape(wide, LANES) for k in range(rows // GRAM_ROWS)], axis=1
    )
    products = lax.dot_general(y, y, (((1,), (1,)), ((), ())), preferred_element_type=jnp.float32)
    row = lax.broadcasted_iota(jnp.int32, products.shape, 0)
    column = lax.broadcasted_iota(jnp.int32, products.shape, 1)
    products = jnp.where((row & (GRAM_ROWS - 1)) == (column & (GRAM_ROWS - 1)), products, 0.0)
    summed = products.reshape(clients, GRAM_ROWS, wide).sum(axis=1)
    owner = lax.broadcasted_iota(jnp.int32, (wide, LANES), 0) // GRAM_ROWS
    lane = lax.broadcasted_iota(jnp.int32, (wide, LANES), 1)
    place = jnp.where((lane & (clients - 1)) == owner, 1.0, 0.0)
    gram = jnp.dot(summed, place, precision=lax.Precision.HIGHEST, preferred_element_type=jnp.float32)
    row = lax.broadcasted_iota(jnp.int32, gram.shape, 0)
    lane = lax.broadcasted_iota(jnp.int32, gram.shape, 1)
    for j in range(out_ref.shape[1]):
        other = (lane - (4 * j + lane // clients)) & (clients - 1)
        diagonals = jnp.where(row == other, gram, 0.0).sum(axis=0, keepdims=True)
        out_ref[:, j] = jnp.broadcast_to(diagonals[None], (out_ref.shape[0], 1, LANES))


def gram_copies(x, copies):
    clients, rows, _ = x.shape
    return pl.pallas_call(
        gram_kernel,
        out_shape=jax.ShapeDtypeStruct((copies, clients // 8 + 1, 1, LANES), jnp.float32),
        compiler_params=params(),
    )(x)


def encode(total):
    values, exponents = [], []
    for at in range(0, BLOCK, SHARED):
        part = total[at : at + SHARED]
        largest = jnp.maximum(jnp.abs(part).max(axis=0, keepdims=True), SMALLEST)
        exponent = jnp.ceil(jnp.log2(largest))
        values.append(jnp.round(part * (TOP * jnp.exp2(-exponent))))
        exponents.append(exponent)
    return jnp.concatenate(values, axis=0).astype(jnp.int32).astype(jnp.int16), exponents


def encode_into(piece_ref, exponent_ref, rows, total_of):
    exponent_ref[...] = jnp.zeros_like(exponent_ref)

    def step(k, carry):
        at = pl.ds(pl.multiple_of(k * BLOCK, BLOCK), BLOCK)
        values, exponents = encode(total_of(at))
        piece_ref[at, :] = values
        for i, exponent in enumerate(exponents):
            exponent_ref[pl.ds(len(exponents) * k + i, 1), :] = exponent
        return carry

    lax.fori_loop(0, rows // BLOCK, step, 0)
    piece_ref[rows : rows + GROUP, :] = exponent_ref[...].astype(jnp.int32).astype(jnp.int16)


def median_kernel(grams_ref, counts_ref, x_ref, piece_ref, safe_ref, beta_ref, exponent_ref):
    clients, rows, _ = x_ref.shape
    summed = jnp.sum(grams_ref[...], axis=0)
    lane = lax.broadcasted_iota(jnp.int32, (clients, LANES), 1)
    row = lax.broadcasted_iota(jnp.int32, (clients, LANES), 0)
    behind = jnp.where(lane < clients, (lane - row) & (clients - 1), clients)
    half = jnp.zeros((clients, LANES), jnp.float32)
    for k in range(clients // 2 + 1):
        diagonal = summed[k // 4]
        if k % 4:
            diagonal = pltpu.roll(diagonal, LANES - clients * (k % 4), 1)
        half = jnp.where(behind == k, diagonal, half)
    identity = jnp.where(lane == row, 1.0, 0.0)
    turned = lax.dot_general(
        half,
        identity,
        (((0,), (0,)), ((), ())),
        precision=lax.Precision.HIGHEST,
        preferred_element_type=jnp.float32,
    )[:clients]
    gram = jnp.where(behind <= clients // 2, half, turned)
    gram = jnp.where(lane < clients, gram, 0.0)
    square = jnp.where(lane == row, gram, 0.0).sum(axis=0, keepdims=True)
    norm = jnp.sqrt(square)

    square_column = jnp.where(lane == row, gram, 0.0).sum(axis=1, keepdims=True)
    counts = counts_ref[...]
    beta, beta_column = counts, jnp.where(lane == row, counts, 0.0).sum(axis=1, keepdims=True)
    share, share_column = beta, beta_column
    safe = jnp.ones((1, 1), jnp.float32)
    for sweep in range(ITERS):
        part = 1.0 / beta.sum(axis=1, keepdims=True)
        inner = (gram * beta_column).sum(axis=0, keepdims=True)
        inner_column = (gram * beta).sum(axis=1, keepdims=True)
        median_square = (inner * beta).sum(axis=1, keepdims=True) * (part * part)
        mean_norm = (norm * beta).sum(axis=1, keepdims=True) * part
        distance = square - (2.0 * part) * inner + median_square + NU_SQUARE
        distance_column = square_column - (2.0 * part) * inner_column + median_square + NU_SQUARE
        scale = norm + mean_norm
        margin = jnp.where(lane[:1] < clients, distance - SAFE_SHARE * (scale * scale), 1.0)
        safe = jnp.minimum(safe, margin.min(axis=1, keepdims=True))
        beta = share / jnp.sqrt(jnp.maximum(distance, NU_SQUARE))
        beta_column = share_column / jnp.sqrt(jnp.maximum(distance_column, NU_SQUARE))
    beta_column = beta_column / beta.sum(axis=1, keepdims=True)
    safe_ref[0] = jnp.where(safe[0, 0] > 0.0, 1, 0)
    beta_ref[...] = jnp.broadcast_to(beta_column, beta_ref.shape)

    def total_of(at):
        total = jnp.zeros((BLOCK, LANES), jnp.float32)
        for c in range(clients):
            total = total + beta_ref[c : c + 1, :] * x_ref[c, at, :].astype(jnp.float32)
        return total

    encode_into(piece_ref, exponent_ref, rows, total_of)


def median_of(grams, counts, x):
    clients, rows, _ = x.shape
    return pl.pallas_call(
        median_kernel,
        out_shape=(
            jax.ShapeDtypeStruct((rows + GROUP, LANES), jnp.int16),
            jax.ShapeDtypeStruct((1,), jnp.int32),
        ),
        out_specs=(pl.BlockSpec(memory_space=pltpu.VMEM), pl.BlockSpec(memory_space=pltpu.SMEM)),
        scratch_shapes=[pltpu.VMEM((clients, LANES), jnp.float32), pltpu.VMEM((GROUP, LANES), jnp.float32)],
        compiler_params=params(),
    )(grams, counts, x)


def update_kernel(parts, ahead, given, first, me_ref, *refs):
    quads, refs = refs[: len(parts)], refs[len(parts) :]
    (momentum_ref, weights_ref), refs = refs[:2], refs[2:]
    given_ref = refs[2] if given else None
    if ahead:
        new_momentum_ref, new_weights_ref, next_ref, held, in_sem, out_sem, next_sem = refs[-7:]
    else:
        new_momentum_ref, new_weights_ref, held, in_sem, out_sem = refs[-5:]
    rows = momentum_ref.shape[1]
    me = me_ref[0]
    x, z = me // (2 * SIDE), (me // 2) % SIDE

    def place(part, near_slot):
        flip, far_slot = part
        core = (me + flip) % 2
        near = jnp.where(core == 1, z, x)
        far = jnp.where(core == 1, x, z)
        near_at = (near + SIDE - near_slot) % SIDE
        far_at = (far + SIDE - far_slot) % SIDE
        return jnp.where(core == 1, far_at * SIDE + near_at, near_at * SIDE + far_at) * 2 + core

    def copies(group, to_ref, sem):
        def fetch(k, near_slot, i):
            slot = SIDE * k + near_slot
            source = (momentum_ref, weights_ref)[i]
            return pltpu.make_async_copy(source.at[place(group[k], near_slot)], to_ref.at[slot, i], sem.at[slot, i])

        return fetch

    def store(k, near_slot, i):
        slot = SIDE * k + near_slot
        target = (new_momentum_ref, new_weights_ref)[i]
        return pltpu.make_async_copy(held.at[slot, i], target.at[place(parts[k], near_slot)], out_sem.at[slot, i])

    def each(k, act):
        def step(near_slot, carry):
            for i in range(2):
                act(k, near_slot, i)
            return carry

        lax.fori_loop(0, SIDE, step, 0)

    fetch = copies(parts, held, in_sem)
    if not given:
        for k in range(len(parts)):
            each(k, lambda *at: fetch(*at).start())
    if ahead:
        fetch_next = copies(ahead, next_ref, next_sem)
        for k in range(len(ahead)):
            each(k, lambda *at: fetch_next(*at).start())
    source_ref, first = (given_ref, SIDE * first) if given else (held, 0)
    for k in range(len(parts)):
        quad = quads[k]

        def work(near_slot, carry):
            slot = SIDE * k + near_slot
            if not given:
                for i in range(2):
                    fetch(k, near_slot, i).wait()
            exponents = quad[near_slot, rows : rows + GROUP, :].astype(jnp.int32).astype(jnp.float32)
            scales = jnp.exp2(exponents) * (1.0 / TOP)
            for at in range(0, rows, BLOCK):
                values = quad[near_slot, at : at + BLOCK, :].astype(jnp.int32).astype(jnp.float32)
                for low in range(0, BLOCK, SHARED):
                    i = (at + low) // SHARED
                    block = pl.ds(at + low, SHARED)
                    median = values[low : low + SHARED] * scales[i : i + 1]
                    moved = MOMENTUM_RATE * source_ref[first + slot, 0, block, :] + median
                    held[slot, 0, block, :] = moved
                    held[slot, 1, block, :] = source_ref[first + slot, 1, block, :] + SERVER_RATE * moved
            for i in range(2):
                store(k, near_slot, i).start()
            return carry

        lax.fori_loop(0, SIDE, work, 0)
    if ahead:
        for k in range(len(ahead)):
            each(k, lambda *at: fetch_next(*at).wait())
    for k in range(len(parts)):
        each(k, lambda *at: store(*at).wait())


def update(parts, me, quads, momentum, weights, made=(), ahead=(), given=None, first=0):
    pieces, rows, _ = momentum.shape
    vmem, hbm = pl.BlockSpec(memory_space=pltpu.VMEM), pl.BlockSpec(memory_space=pltpu.HBM)
    shape = pltpu.HBM(momentum.shape, momentum.dtype)
    in_hbm = [pltpu.with_memory_space_constraint(array, pltpu.HBM) for array in (momentum, weights, *made)]
    in_vmem = [] if given is None else [pltpu.with_memory_space_constraint(given, pltpu.VMEM)]
    slots, next_slots = SIDE * len(parts), SIDE * len(ahead)
    pair = (2, rows, LANES)
    sems = pltpu.SemaphoreType.DMA((slots, 2))
    more = bool(ahead)
    return pl.pallas_call(
        lambda *refs: update_kernel(parts, ahead, given is not None, first, *refs),
        in_specs=[pl.BlockSpec(memory_space=pltpu.SMEM)] + [vmem] * len(quads) + [hbm] * 2 + [hbm] * len(made)
        + [vmem] * len(in_vmem),
        out_specs=(hbm, hbm) + (vmem,) * more,
        out_shape=(shape, shape) + (pltpu.VMEM((next_slots, *pair), jnp.float32),) * more,
        scratch_shapes=[pltpu.VMEM((slots, *pair), jnp.float32), sems, sems]
        + [pltpu.SemaphoreType.DMA((next_slots, 2))] * more,
        input_output_aliases={1 + len(quads) + 2 + i: i for i in range(len(made))},
        compiler_params=params(),
        cost_estimate=pl.CostEstimate(flops=1, bytes_accessed=1, transcendentals=0),
    )(me, *quads, *in_hbm, *in_vmem)


def along(step, shift):
    pairs = []
    for x in range(SIDE):
        for z in range(SIDE):
            for core in range(2):
                if (core == 1) == (step == 0):
                    to_x, to_z = x, (z + shift) % SIDE
                else:
                    to_x, to_z = (x + shift) % SIDE, z
                pairs.append(((x * SIDE + z) * 2 + core, (to_x * SIDE + to_z) * 2 + core))
    return pairs


def direct(x, counts):
    share = counts / jnp.sum(counts)
    wide = x.astype(jnp.float32)

    def weighted(coefficients):
        return jnp.sum(coefficients[:, None, None] * wide, axis=0)

    median = weighted(share)
    for sweep in range(ITERS):
        squared = lax.psum(jnp.sum(jnp.square(wide - median[None]), axis=(1, 2)), ("wide", "narrow"))
        beta = share / jnp.sqrt(squared + NU_SQUARE)
        median = weighted(beta) / jnp.sum(beta)
    copies = jnp.broadcast_to(median[None], x.shape)
    return lax.all_to_all(copies, "wide", split_axis=0, concat_axis=0, tiled=True)


def shards(deltas, sample_counts, momentum, weights):
    clients = sample_counts.shape[0]
    counts = sample_counts.astype(jnp.float32)
    padded = jnp.pad(counts, (0, LANES - clients)).reshape(1, LANES)
    me = lax.axis_index("wide").astype(jnp.int32).reshape(1)
    x = lax.all_to_all(pack(deltas, clients), "wide", split_axis=0, concat_axis=0, tiled=True)
    devices = lax.axis_size(("wide", "narrow"))
    grams = lax.all_to_all(gram_copies(x, devices), ("wide", "narrow"), split_axis=0, concat_axis=0, tiled=True)
    flat = momentum.shape
    blocks = (clients, momentum.shape[0] // clients // LANES, LANES)
    momentum, weights = momentum.reshape(blocks), weights.reshape(blocks)
    piece, safe = median_of(grams, padded, x)

    near = [piece] + [lax.ppermute(piece, "wide", along(0, shift)) for shift in range(1, SIDE)]
    own = jnp.stack(near)
    ours = [own] + [lax.ppermute(own, "wide", along(1, shift)) for shift in range(1, SIDE)]
    across = [(i, i ^ 1) for i in range(2 * SIDE * SIDE)]
    theirs = lax.ppermute(own, "wide", across)
    first, second = (lax.ppermute(own, "wide", along(1, shift)) for shift in (1, 3))
    made = update([(0, 0), (1, 0)], me, [own, theirs], momentum, weights)
    again_own, *made = lax.optimization_barrier((own, *made))
    last = lax.ppermute(again_own, "wide", along(1, 2))
    rest = [(0, 3), (1, 1), (1, 3), (0, 2), (1, 2)]
    first, *made = lax.optimization_barrier((first, *made))
    theirs = [lax.ppermute(first, "wide", across)]
    *made, given = update([(0, 1)], me, [first], momentum, weights, made, ahead=rest)
    second, *made = lax.optimization_barrier((second, *made))
    theirs = theirs + [lax.ppermute(second, "wide", across)]
    made = update(rest[:1], me, [second], momentum, weights, made, given=given)
    last, *made = lax.optimization_barrier((last, *made))
    theirs = theirs + [lax.ppermute(last, "wide", across)]
    made = update(rest[1:3], me, theirs[:2], momentum, weights, made, given=given, first=1)
    new_momentum, new_weights = update(rest[3:], me, [last, theirs[2]], momentum, weights, made, given=given, first=3)

    def again(state):
        new_momentum = MOMENTUM_RATE * momentum + direct(x, counts)
        return jnp.int32(1), new_momentum, weights + SERVER_RATE * new_momentum

    state = (safe[0], new_momentum, new_weights)
    _, new_momentum, new_weights = lax.while_loop(lambda state: state[0] == 0, again, state)
    return (new_weights.reshape(flat), new_momentum.reshape(flat))


def solution(mesh):
    placed = (P("wide", "narrow"), P(), P("narrow"), P("narrow"))
    return jax.shard_map(
        shards, mesh=mesh, in_specs=placed, out_specs=(P("narrow"), P("narrow")), check_vma=False
    )
```
